32 devices in a mesh: groups: 2 (over x), seq: 16 (over z, y, core).
Axes of the slice: x: 2, y: 2, z: 4, core: 2. Of those that a mesh axis runs over, the one named last changes fastest.
Arguments:
- tile_heads: bfloat16 [8192, 1536], P(('groups', 'seq')), parts along dimension 0, may hold values from -6 to 6
- tile_stream: bfloat16 [8192, 1536], P(('groups', 'seq')), parts along dimension 0, may hold values from -6 to 6
- tissue_counts: int32 [32], P('groups'), parts along dimension 0, may hold values from 1 to 256, 2048 in all
- head_weight: bfloat16 [1536, 1536], replicated, may hold values from -0.15625 to 0.15625
- stream_scale: float32 [1536], replicated, may hold values from 0.3 to 3
- final_gain: float32 [1536], replicated, may hold values from 0.1 to 1.9
- final_bias: float32 [1536], replicated, may hold values from -3 to 3
- embed_weight: bfloat16 [1536, 768], replicated, may hold values from -0.15625 to 0.15625
- embed_bias: float32 [768], replicated, may hold values from -3 to 3
- slide_gain: float32 [768], replicated, may hold values from 0.1 to 1.9
- triple_weight: bfloat16 [768, 1152], replicated, may hold values from -4 to 4
- inner_gain: float32 [384], replicated, may hold values from 0.1 to 1.9
- output_weight: bfloat16 [384, 768], replicated, may hold values from -0.3125 to 0.3125
Outputs:
- attended: bfloat16 [4096, 768], P(('groups', 'seq')), parts along dimension 0
The draws below stay inside these ranges and needn't reach their ends.
There are 2 independent parts, one for each index of `groups`. The reference program is written for one: setup_inputs(seed, part) draws one part's arguments, and reference() takes and returns one part's arrays. A program takes and returns all parts, laid end to end along the dimension named above; an argument that names none is the same for every part. Nothing has to cross between parts.
Inputs may be any that keep to these rules, and one draw needn't show every extreme that they name: `tissue_counts`: the counts sum to 2048; some loader holds exactly 256 tiles.
All inputs are finite; a program needn't handle non-finite values.
Results may differ from the reference program's by a relative error of at most 0.017.
Values may be sent and summed in bfloat16 or wider, within the bound.
A program may use at most 128 MiB of HBM per device.

```python
import math
import jax
import jax.numpy as jnp
import numpy as np
from jax import lax

DT = 1536
DS = 768
HEAD_DIM = 48
HEADS = 8
BRANCHES = 5
SEG_BASE = 1024
TILE_DEV = 128
LOAD_DEV = 256
N_SEQ = 16


def draw_triple_weight(key, part):
    key = jax.random.fold_in(key, 7)
    inner_width = HEADS * HEAD_DIM
    query_key, noise_key, value_key = jax.random.split(key, 3)
    query_part = jax.random.normal(query_key, (DS, inner_width), jnp.float32)
    noise_part = jax.random.normal(noise_key, (DS, inner_width), jnp.float32)
    value_part = jax.random.normal(value_key, (DS, inner_width), jnp.float32) / math.sqrt(DS)
    query_part = query_part * 1.3 / math.sqrt(DS)
    key_part = noise_part * 1.3 / math.sqrt(DS)
    joined = jnp.concatenate([query_part, key_part, value_part], axis=1)
    return jnp.clip(joined, -4.0, 4.0).astype(jnp.bfloat16)


def level_of(own_key, shape, cuts, low, high):
    level, own = 1.0, jax.random.fold_in(own_key, 6)
    for dim, blocks in cuts:
        heights = jnp.exp(jax.random.uniform(jax.random.fold_in(own, dim), (blocks,), jnp.float32, low / len(cuts), high / len(cuts)))
        level = level * jnp.repeat(heights, shape[dim] // blocks).reshape([-1 if axis == dim else 1 for axis in range(len(shape))])
    return level


def split_up(amount, total, limit, slope):
    loads = [(1 << 20) // math.isqrt(grade ** slope) + 1 for grade in range(2, amount + 1)]
    surplus, holding = total - limit - (amount - 1), [1] * (amount - 1)
    while surplus > 0:
        movable = [i for i in range(amount - 1) if holding[i] < limit]
        pool, remaining = sum([loads[i] for i in movable]), surplus
        for i in movable:
            extra = min(limit - holding[i], max(1, remaining * loads[i] // pool), surplus)
            holding[i] = holding[i] + extra
            surplus = surplus - extra
    return np.array([limit] + holding)


def uneven(key, count, total, most, lean):
    if count == 2:
        one = jax.random.randint(key, (), max(1, total - most), min(most, total - 1) + 1)
        return jnp.stack([one, total - one])
    sizes = jnp.asarray(split_up(count, total, most, lean), jnp.int32)
    couples = (count - 1) // 2
    giver, receiver = sizes[1:1 + 2 * couples:2], sizes[2:2 + 2 * couples:2]
    room = jnp.minimum(giver - 1, most - receiver)
    shifted = jax.random.randint(jax.random.fold_in(key, 1), (couples,), 0, 1 << 20) % (room + 1)
    sizes = sizes.at[1:1 + 2 * couples:2].set(giver - shifted).at[2:2 + 2 * couples:2].set(receiver + shifted)
    return sizes[jax.random.permutation(jax.random.fold_in(key, 2), count)]


def gaussian(stream_key, dims, width, most, pieces=(), kind=jnp.bfloat16):
    array = jax.random.normal(stream_key, dims, jnp.float32) * width
    if len(pieces) > 0:
        array = level_of(stream_key, dims, pieces, -0.22, 0.18) * array
    return jnp.clip(array, min=-most, max=most).astype(kind)


def setup_inputs(seed: int = 0, part: int = 0) -> dict:
    splits = jax.random.split(jax.random.key(seed), 14)
    own_keys = jax.random.split(jax.random.fold_in(splits[13], part), 14)
    return {
        "tile_heads": gaussian(own_keys[0], (N_SEQ * LOAD_DEV, DT), 1.0, 6.0, ((0, 16),)),
        "tile_stream": gaussian(own_keys[1], (N_SEQ * LOAD_DEV, DT), 1.0, 6.0, ((0, 16),)),
        "tissue_counts": uneven(own_keys[2], N_SEQ, TILE_DEV * N_SEQ, LOAD_DEV, 2).astype(jnp.int32),
        "head_weight": gaussian(splits[3], (DT, DT), DT ** -0.5, 0.15625),
        "stream_scale": jnp.clip(jnp.exp(jax.random.uniform(splits[4], (DT,), jnp.float32, math.log(0.3), math.log(3.0))), 0.3, 3.0),
        "final_gain": jnp.clip(1.0 + 0.18 * jax.random.normal(splits[5], (DT,), jnp.float32), 0.1, 1.9),
        "final_bias": gaussian(splits[6], (DT,), 0.5, 3.0, (), jnp.float32),
        "embed_weight": gaussian(splits[7], (DT, DS), DT ** -0.5, 0.15625),
        "embed_bias": gaussian(splits[8], (DS,), 0.5, 3.0, (), jnp.float32),
        "slide_gain": jnp.clip(1.0 + 0.18 * jax.random.normal(splits[9], (DS,), jnp.float32), 0.1, 1.9),
        "triple_weight": draw_triple_weight(jax.random.fold_in(splits[13], 71), part),
        "inner_gain": jnp.clip(1.0 + 0.18 * jax.random.normal(splits[11], (HEADS * HEAD_DIM,), jnp.float32), 0.1, 1.9),
        "output_weight": gaussian(splits[12], (HEADS * HEAD_DIM, DS), (HEADS * HEAD_DIM) ** -0.5, 0.3125),
    }


EPSILON = 1e-06
NEGATIVE = -1e+30

def layer_norm(values, gain_vector):
    average = lax.optimization_barrier(jnp.mean(values, axis=-1, keepdims=True))
    centred = values - average
    spread = lax.optimization_barrier(jnp.mean(centred * centred, axis=-1, keepdims=True))
    return centred * lax.rsqrt(spread + EPSILON) * gain_vector

def encode(head_rows, stream_rows, head_weight, stream_scale, final_gain, final_bias):
    blended = jnp.dot(head_rows, head_weight, preferred_element_type=jnp.float32)
    summed = stream_rows.astype(jnp.float32) + stream_scale * blended
    return (layer_norm(summed, final_gain) + final_bias).astype(jnp.bfloat16)

def segment_attend(triple):
    query_rows, key_rows, value_rows = triple
    scaling = 1.0 / math.sqrt(query_rows.shape[-1])
    scores = jnp.dot(query_rows, key_rows.T, preferred_element_type=jnp.float32) * scaling
    highest = lax.optimization_barrier(jnp.max(scores, axis=1))
    weights = jnp.exp(scores - highest[:, None])
    totals = lax.optimization_barrier(jnp.sum(weights, axis=1))
    blended = jnp.dot(weights.astype(jnp.bfloat16), value_rows, preferred_element_type=jnp.float32)
    return (highest, totals, blended)

def dilated_attention(queries, key_rows, value_rows):
    length, head_count, head_width = queries.shape
    high_list, total_list, mix_list = ([], [], [])
    for branch in range(BRANCHES):
        stride = 2 ** branch
        segment = min(SEG_BASE * stride, length)
        picked = length // stride
        head_high, head_total, head_mix = ([], [], [])
        for head_index in range(head_count):
            offset = head_index % stride

            def select_rows(source):
                return source[:, head_index].reshape(length // segment, segment // stride, stride, head_width)[:, :, offset]
            highest, summed, blended = lax.map(segment_attend, (select_rows(queries), select_rows(key_rows), select_rows(value_rows)))
            head_high.append(jnp.full((picked, stride), NEGATIVE, jnp.float32).at[:, offset].set(highest.reshape(picked)).reshape(length))
            head_total.append(jnp.zeros((picked, stride), jnp.float32).at[:, offset].set(summed.reshape(picked)).reshape(length))
            head_mix.append(jnp.zeros((picked, stride, head_width), jnp.float32).at[:, offset].set(blended.reshape(picked, head_width)).reshape(length, head_width))
        high_list.append(jnp.stack(head_high, axis=1))
        total_list.append(jnp.stack(head_total, axis=1))
        mix_list.append(jnp.stack(head_mix, axis=1))
    high_all = jnp.stack(high_list)
    summit = lax.optimization_barrier(jnp.max(high_all, axis=0))
    factor = jnp.exp(high_all - summit)
    denominator = lax.optimization_barrier(jnp.sum(jnp.stack(total_list) * factor, axis=0))
    numerator = lax.optimization_barrier(jnp.sum(jnp.stack(mix_list) * factor[..., None], axis=0))
    return (numerator / denominator[..., None]).reshape(length, head_count * head_width)

def reference(tile_heads, tile_stream, tissue_counts, head_weight, stream_scale, final_gain, final_bias, embed_weight, embed_bias, slide_gain, triple_weight, inner_gain, output_weight):
    devices = N_SEQ
    load_rows = tile_heads.shape[0] // devices
    total_rows = devices * TILE_DEV
    starts = (jnp.cumsum(tissue_counts) - tissue_counts).astype(jnp.int32)
    slot_ids = jnp.arange(load_rows, dtype=jnp.int32)
    filled = slot_ids[None, :] < tissue_counts[:, None]
    position = starts[:, None] + slot_ids[None, :]
    target = jnp.where(filled, position, total_rows).reshape(devices * load_rows).astype(jnp.int32)
    source = jnp.zeros((total_rows,), jnp.int32).at[target].set(jnp.arange(devices * load_rows, dtype=jnp.int32), mode='drop')
    embedding = encode(tile_heads[source], tile_stream[source], head_weight, stream_scale, final_gain, final_bias)
    slide_rows = (jnp.dot(embedding, embed_weight, preferred_element_type=jnp.float32) + embed_bias).astype(jnp.bfloat16)
    normed = layer_norm(slide_rows.astype(jnp.float32), slide_gain).astype(jnp.bfloat16)
    triple = jnp.dot(normed, triple_weight, preferred_element_type=jnp.float32).astype(jnp.bfloat16)
    inner_width = HEADS * HEAD_DIM
    queries = triple[:, :inner_width].reshape(total_rows, HEADS, HEAD_DIM)
    key_rows = triple[:, inner_width:2 * inner_width].reshape(total_rows, HEADS, HEAD_DIM)
    value_rows = triple[:, 2 * inner_width:].reshape(total_rows, HEADS, HEAD_DIM)
    blended = dilated_attention(queries, key_rows, value_rows)
    inner = layer_norm(blended, inner_gain).astype(jnp.bfloat16)
    return jnp.dot(inner, output_weight, preferred_element_type=jnp.float32).astype(jnp.bfloat16)
```

```python
import math

import jax
import jax.numpy as jnp
import numpy as np
from jax import lax
from jax.experimental import pallas as pl
from jax.experimental.pallas import tpu as pltpu
from jax.sharding import PartitionSpec as P

HEAD_DIM = 48
HEADS = 8
BRANCHES = 5
SEG_BASE = 1024
TILE_DEV = 128


EPSILON = 1e-06
NEGATIVE = -1e30


def swapped(block, axis, stride):
    count = lax.axis_size(axis)
    route = []
    for low in range(count):
        high = low | 1 << stride
        if high != low and high < count:
            route += [(low, high), (high, low)]
    return lax.ppermute(block, axis, route)


def layer_norm(values, gain_vector):
    average = jnp.mean(values, axis=-1, keepdims=True)
    centred = values - average
    spread = jnp.mean(centred * centred, axis=-1, keepdims=True)
    return centred * lax.rsqrt(spread + EPSILON) * gain_vector


def encode(head_rows, stream_rows, head_weight, stream_scale, final_gain, final_bias):
    blended = jnp.dot(head_rows, head_weight, preferred_element_type=jnp.float32)
    summed = stream_rows.astype(jnp.float32) + stream_scale * blended
    return (layer_norm(summed, final_gain) + final_bias).astype(jnp.bfloat16)


def project(embedding, embed_weight, embed_bias):
    return (
        jnp.dot(embedding, embed_weight, preferred_element_type=jnp.float32) + embed_bias
    ).astype(jnp.bfloat16)


def member_table(stride):
    return np.arange(stride)[:, None] == (np.arange(HEADS) % stride)[None, :]


def select_heads(source, stride):
    shaped = source.reshape(source.shape[0] // stride, stride, HEADS, source.shape[-1])
    member = member_table(stride)[None, :, :, None]
    return jnp.sum(jnp.where(member, shaped, jnp.zeros((), shaped.dtype)), axis=1)


def spread_heads(values, stride, fill_value):
    member = member_table(stride)
    if values.ndim == 3:
        member = member[:, :, None]
    member = member[None]
    placed = jnp.where(member, values[:, None], jnp.asarray(fill_value, values.dtype))
    return placed.reshape((values.shape[0] * stride,) + values.shape[1:])


def local_general(
    tile_heads,
    tile_stream,
    tissue_counts,
    head_weight,
    stream_scale,
    final_gain,
    final_bias,
    embed_weight,
    embed_bias,
    slide_gain,
    triple_weight,
    inner_gain,
    output_weight,
):
    devices = lax.axis_size("seq")
    rank_here = lax.axis_index("seq")
    capacity = tile_heads.shape[0] // devices
    per_peer = TILE_DEV // devices
    starts = jnp.cumsum(tissue_counts) - tissue_counts
    own_start = starts[rank_here]

    def outbound(source):
        shaped = source.reshape(capacity, devices, source.shape[-1])
        return jnp.roll(shaped, own_start % devices, axis=1)

    column = jnp.remainder(rank_here - starts, devices)
    slot_ids = jnp.arange(capacity, dtype=jnp.int32)[:, None] * devices + column[None, :]
    filled = slot_ids < tissue_counts[None, :]
    home_slot = (starts[None, :] + slot_ids) // devices
    target = jnp.where(filled, home_slot, TILE_DEV).reshape(capacity * devices)

    def place_rows(arrived):
        flattened = arrived.reshape(capacity * devices, arrived.shape[-1])
        return (
            jnp.zeros((TILE_DEV, flattened.shape[-1]), flattened.dtype)
            .at[target]
            .set(flattened, mode="drop")
        )

    head_in, stream_in = (
        lax.all_to_all(outbound(tile_heads), "seq", split_axis=1, concat_axis=1, tiled=True),
        lax.all_to_all(outbound(tile_stream), "seq", split_axis=1, concat_axis=1, tiled=True),
    )
    embedding = encode(
        place_rows(head_in),
        place_rows(stream_in),
        head_weight,
        stream_scale,
        final_gain,
        final_bias,
    )
    back_home = lax.all_to_all(
        embedding.reshape(devices, per_peer, 1, embedding.shape[-1]),
        "seq",
        split_axis=0,
        concat_axis=2,
        tiled=True,
    )
    slide_rows = project(back_home.reshape(TILE_DEV, embedding.shape[-1]), embed_weight, embed_bias)
    normed = layer_norm(slide_rows.astype(jnp.float32), slide_gain).astype(jnp.bfloat16)
    triple = jnp.dot(normed, triple_weight, preferred_element_type=jnp.float32).astype(jnp.bfloat16)
    inner_width = HEADS * HEAD_DIM
    queries = triple[:, :inner_width].reshape(TILE_DEV, HEADS, HEAD_DIM)
    key_value = jnp.concatenate(
        [
            triple[:, inner_width : 2 * inner_width].reshape(TILE_DEV, HEADS, HEAD_DIM),
            triple[:, 2 * inner_width :].reshape(TILE_DEV, HEADS, HEAD_DIM),
        ],
        axis=2,
    )
    total_rows = TILE_DEV * devices
    strides = [2**branch for branch in range(BRANCHES)]
    depths = [
        (min(SEG_BASE * stride, total_rows) // TILE_DEV).bit_length() - 1 for stride in strides
    ]
    blocks = [
        select_heads(key_value, stride).reshape(TILE_DEV // stride, 2 * inner_width)
        for stride in strides
    ]
    gathered = []
    for branch in range(BRANCHES):
        current = blocks[branch]
        for bit_place in range(depths[branch]):
            partner = swapped(current, "seq", bit_place)
            current = jnp.concatenate([current, partner], axis=0)
        gathered.append(current)
    scaling = 1.0 / math.sqrt(HEAD_DIM)
    high_list, total_list, mix_list = ([], [], [])
    for branch in range(BRANCHES):
        stride = strides[branch]
        own_queries = select_heads(queries, stride)
        gathered_rows = gathered[branch].reshape(-1, HEADS, 2 * HEAD_DIM)
        scores = (
            jnp.einsum(
                "qhd,khd->hqk",
                own_queries,
                gathered_rows[:, :, :HEAD_DIM],
                preferred_element_type=jnp.float32,
            )
            * scaling
        )
        highest = jnp.max(scores, axis=2)
        weights = jnp.exp(scores - highest[:, :, None])
        summed = jnp.sum(weights, axis=2)
        blended = jnp.einsum(
            "hqk,khd->qhd",
            weights.astype(jnp.bfloat16),
            gathered_rows[:, :, HEAD_DIM:],
            preferred_element_type=jnp.float32,
        )
        high_list.append(spread_heads(highest.T, stride, NEGATIVE))
        total_list.append(spread_heads(summed.T, stride, 0.0))
        mix_list.append(spread_heads(blended, stride, 0.0))
    high_all = jnp.stack(high_list)
    summit = jnp.max(high_all, axis=0)
    factor = jnp.exp(high_all - summit)
    denominator = jnp.sum(jnp.stack(total_list) * factor, axis=0)
    numerator = jnp.sum(jnp.stack(mix_list) * factor[..., None], axis=0)
    mixed = (numerator / denominator[..., None]).reshape(TILE_DEV, inner_width)
    inner = layer_norm(mixed, inner_gain).astype(jnp.bfloat16)
    return jnp.dot(inner, output_weight, preferred_element_type=jnp.float32).astype(jnp.bfloat16)


MESH = pl.DeviceIdType.MESH
PIECE = 3 * HEAD_DIM
HALF = 1024
NT = (((1,), (1,)), ((), ()))
TN = (((0,), (0,)), ((), ()))
F32 = jnp.float32
BF16 = jnp.bfloat16
MIB = 2**20


def encode_kernel(
    heads_ref,
    stream_ref,
    scale_ref,
    gain_ref,
    bias_ref,
    embed_bias_ref,
    slide_gain_ref,
    head_weight_hbm,
    embed_weight_hbm,
    triple_weight_hbm,
    recv_ref,
    head_weight,
    embed_weight,
    triple_weight,
    outbox,
    load_sem,
    own_sem,
    send_sem,
    pass_sem,
    recv_sem,
):
    group = lax.axis_index("groups")
    me = lax.axis_index("seq")
    chip, core = me // 2, lax.rem(me, 2)
    sibling = 2 * chip + 1 - core
    chips = HEADS
    depth = head_weight.shape[0]
    part = depth // 4
    loads = [
        pltpu.make_async_copy(
            head_weight_hbm.at[pl.ds(i * part, part)],
            head_weight.at[pl.ds(i * part, part)],
            load_sem.at[i],
        )
        for i in range(4)
    ]
    loads.append(pltpu.make_async_copy(embed_weight_hbm, embed_weight, load_sem.at[4]))
    loads.append(pltpu.make_async_copy(triple_weight_hbm, triple_weight, load_sem.at[5]))
    for load in loads:
        load.start()

    barrier = pltpu.get_barrier_semaphore()
    for off in range(1, chips):
        peer = 2 * lax.rem(chip + off, chips) + core
        pl.semaphore_signal(barrier, inc=1, device_id=(group, peer), device_id_type=MESH)
    pl.semaphore_signal(barrier, inc=1, device_id=(group, sibling), device_id_type=MESH)

    blended = None
    for i in range(4):
        loads[i].wait()
        term = jnp.dot(
            heads_ref[:, i * part : (i + 1) * part],
            head_weight[i * part : (i + 1) * part, :],
            preferred_element_type=F32,
        )
        blended = term if blended is None else blended + term
    summed = stream_ref[...].astype(F32) + scale_ref[...] * blended
    embedding = (layer_norm(summed, gain_ref[...]) + bias_ref[...]).astype(BF16)
    loads[4].wait()
    slide_rows = (
        jnp.dot(embedding, embed_weight[...], preferred_element_type=F32) + embed_bias_ref[...]
    ).astype(BF16)
    normed = layer_norm(slide_rows.astype(F32), slide_gain_ref[...]).astype(BF16)
    loads[5].wait()
    triple = jnp.dot(normed, triple_weight[...], preferred_element_type=F32)
    turned = triple.T.astype(BF16)
    inner = HEADS * HEAD_DIM
    for h in range(HEADS):
        for kind in range(3):
            low = kind * inner + h * HEAD_DIM
            outbox[h, kind * HEAD_DIM : (kind + 1) * HEAD_DIM, :] = turned[low : low + HEAD_DIM, :]

    pl.semaphore_wait(barrier, chips)
    sends = []
    for off in range(1, chips):
        to = lax.rem(chip + off, chips)
        copy = pltpu.make_async_remote_copy(
            src_ref=outbox.at[to],
            dst_ref=recv_ref.at[me],
            send_sem=send_sem.at[off],
            recv_sem=recv_sem.at[me],
            device_id=(group, 2 * to + core),
            device_id_type=MESH,
        )
        copy.start()
        sends.append(copy)
    copy = pltpu.make_async_remote_copy(
        src_ref=outbox.at[chip],
        dst_ref=recv_ref.at[me],
        send_sem=send_sem.at[0],
        recv_sem=recv_sem.at[me],
        device_id=(group, sibling),
        device_id_type=MESH,
    )
    copy.start()
    sends.append(copy)
    own = pltpu.make_async_copy(outbox.at[chip], recv_ref.at[me], own_sem)
    own.start()
    for off in range(1, chips):
        source = 2 * lax.rem(chip + chips - off, chips) + core
        onward = pltpu.make_async_remote_copy(
            src_ref=recv_ref.at[source],
            dst_ref=recv_ref.at[source],
            send_sem=pass_sem.at[off],
            recv_sem=recv_sem.at[source],
            device_id=(group, sibling),
            device_id_type=MESH,
        )
        onward.wait_recv()
        onward.start()
        sends.append(onward)
    for off in range(chips):
        source = 2 * lax.rem(chip + chips - off, chips) + 1 - core
        pltpu.make_async_remote_copy(
            src_ref=recv_ref.at[source],
            dst_ref=recv_ref.at[source],
            send_sem=pass_sem.at[0],
            recv_sem=recv_sem.at[source],
            device_id=(group, sibling),
            device_id_type=MESH,
        ).wait_recv()
    for copy in sends:
        copy.wait_send()
    own.wait()


def shared_depth(index, shift):
    residue = (index + 8 - shift) & 7
    depth = jnp.where(residue & 4 != 0, 3, 4)
    depth = jnp.where(residue & 2 != 0, 2, depth)
    return jnp.where(residue & 1 != 0, 1, depth)


def attend(keys, queries, multiplicity):
    scaling = 1.0 / math.sqrt(HEAD_DIM)
    scores = [
        lax.dot_general(block, queries, NT, preferred_element_type=F32) for block in keys
    ]
    highest = scores[0].max(axis=0, keepdims=True)
    for block in scores[1:]:
        highest = jnp.maximum(highest, block.max(axis=0, keepdims=True))
    total = blended = None
    for block, values, times in zip(scores, keys, multiplicity):
        weights = jnp.exp((block - highest) * scaling)
        if times is not None:
            weights = weights * times
        part_total = weights.sum(axis=0, keepdims=True)
        part = lax.dot_general(values, weights.astype(BF16), TN, preferred_element_type=F32)
        total = part_total if total is None else total + part_total
        blended = part if blended is None else blended + part
    return blended[2 * HEAD_DIM : PIECE, :] / total


def attention_kernel(counts_ref, pieces_ref, out_ref, left, right):
    me = lax.axis_index("seq")
    head, side = me // 2, lax.rem(me, 2)
    parity, shift = lax.rem(head, 2), head // 2
    slots = pieces_ref.shape[2]
    unit = (
        lax.broadcasted_iota(jnp.int32, (slots, slots), 0)
        == lax.broadcasted_iota(jnp.int32, (slots, slots), 1)
    ).astype(BF16)
    right[...] = jnp.zeros_like(right)
    start = 0
    for d in range(pieces_ref.shape[0]):
        rows = lax.dot_general(unit, pieces_ref[d], NT, preferred_element_type=F32)
        left[pl.ds(start, slots), :] = rows[:, :128]
        right[pl.ds(start, slots), : PIECE - 128] = rows[:, 128:]
        start = start + counts_ref[d]

    def pick(first, which):
        place = pl.ds(first + which, HALF // 2, stride=2)
        return jnp.concatenate(
            [left[place, :].astype(BF16), right[place, :].astype(BF16)], axis=1
        )

    def as_queries(rows):
        lane = lax.broadcasted_iota(jnp.int32, (HALF // 2, 128), 1)
        kept = jnp.where(lane < HEAD_DIM, rows[:, :128].astype(F32), 0.0)
        moved = pltpu.roll(kept, HEAD_DIM, 1).astype(BF16)
        return jnp.concatenate([moved, jnp.zeros_like(moved)], axis=1)

    near = pick(side * HALF, parity)
    near_off = pick(side * HALF, 1 - parity)
    far = pick((1 - side) * HALF, parity)
    count = HALF // 2
    key_depth = shared_depth(lax.broadcasted_iota(jnp.int32, (count, 1), 0), shift)
    query_depth = shared_depth(lax.broadcasted_iota(jnp.int32, (1, count), 1), shift)
    times = jnp.minimum(key_depth, query_depth).astype(F32)
    same = attend([near, near_off, far], as_queries(near), [times + 1.0, None, times])
    off = attend([near, near_off], as_queries(near_off), [None, None])
    even = jnp.where(parity == 0, same, off).astype(BF16)
    odd = jnp.where(parity == 0, off, same).astype(BF16)
    for t in range(HALF // TILE_DEV):
        low = t * (TILE_DEV // 2)
        out_ref[t] = jnp.concatenate(
            [even[:, low : low + TILE_DEV // 2], odd[:, low : low + TILE_DEV // 2]], axis=1
        )


def project_kernel(tiles_ref, gain_ref, weight_ref, out_ref, inbox, own_sem, send_sem, recv_sem):
    group = lax.axis_index("groups")
    me = lax.axis_index("seq")
    devices = 2 * HEADS
    barrier = pltpu.get_barrier_semaphore()
    for off in range(1, devices):
        peer = lax.rem(me + off, devices)
        pl.semaphore_signal(barrier, inc=1, device_id=(group, peer), device_id_type=MESH)
    pl.semaphore_wait(barrier, devices - 1)
    head, side = me // 2, lax.rem(me, 2)
    home_side = me // HEADS

    def remote(t):
        return pltpu.make_async_remote_copy(
            src_ref=tiles_ref.at[t],
            dst_ref=inbox.at[head],
            send_sem=send_sem.at[t],
            recv_sem=recv_sem.at[head],
            device_id=(group, side * HEADS + t),
            device_id_type=MESH,
        )

    for t in range(HEADS):

        @pl.when(side * HEADS + t != me)
        def _():
            remote(t).start()

        @pl.when(side * HEADS + t == me)
        def _():
            own = pltpu.make_async_copy(tiles_ref.at[t], inbox.at[head], own_sem)
            own.start()
            own.wait()

    for h in range(HEADS):

        @pl.when(2 * h + home_side != me)
        def _():
            pltpu.make_async_remote_copy(
                src_ref=tiles_ref.at[0],
                dst_ref=inbox.at[h],
                send_sem=send_sem.at[0],
                recv_sem=recv_sem.at[h],
                device_id=(group, 2 * h + home_side),
                device_id_type=MESH,
            ).wait_recv()

    mixed = inbox[...].astype(F32).reshape(HEADS * HEAD_DIM, TILE_DEV)
    average = jnp.mean(mixed, axis=0, keepdims=True)
    centred = mixed - average
    spread = jnp.mean(centred * centred, axis=0, keepdims=True)
    inner = (centred * lax.rsqrt(spread + EPSILON) * gain_ref[...]).astype(BF16)
    row = lax.broadcasted_iota(jnp.int32, (TILE_DEV, TILE_DEV), 0)
    lane = lax.broadcasted_iota(jnp.int32, (TILE_DEV, TILE_DEV), 1)
    half = TILE_DEV // 2
    order = (row == 2 * lax.rem(lane, half) + lane // half).astype(BF16)
    rows = lax.dot_general(order, inner, NT, preferred_element_type=F32).astype(BF16)
    out_ref[...] = jnp.dot(rows, weight_ref[...], preferred_element_type=F32).astype(BF16)
    for t in range(HEADS):

        @pl.when(side * HEADS + t != me)
        def _():
            remote(t).wait_send()


def local(
    tile_heads,
    tile_stream,
    tissue_counts,
    head_weight,
    stream_scale,
    final_gain,
    final_bias,
    embed_weight,
    embed_bias,
    slide_gain,
    triple_weight,
    inner_gain,
    output_weight,
):
    devices = lax.axis_size("seq")
    if devices != 2 * HEADS:
        return local_general(
            tile_heads,
            tile_stream,
            tissue_counts,
            head_weight,
            stream_scale,
            final_gain,
            final_bias,
            embed_weight,
            embed_bias,
            slide_gain,
            triple_weight,
            inner_gain,
            output_weight,
        )
    slots = tile_heads.shape[0]
    vmem = pl.BlockSpec(memory_space=pltpu.VMEM)
    smem = pl.BlockSpec(memory_space=pltpu.SMEM)
    hbm = pl.BlockSpec(memory_space=pl.ANY)
    dma = pltpu.SemaphoreType.DMA
    pieces = pl.pallas_call(
        encode_kernel,
        out_shape=jax.ShapeDtypeStruct((devices, PIECE, slots), BF16),
        in_specs=[vmem] * 7 + [hbm] * 3,
        out_specs=hbm,
        scratch_shapes=[
            pltpu.VMEM(head_weight.shape, BF16),
            pltpu.VMEM(embed_weight.shape, BF16),
            pltpu.VMEM(triple_weight.shape, BF16),
            pltpu.VMEM((HEADS, PIECE, slots), BF16),
            dma((6,)),
            dma,
            dma((HEADS,)),
            dma((HEADS,)),
            dma((devices,)),
        ],
        compiler_params=pltpu.CompilerParams(
            collective_id=0, has_side_effects=True, vmem_limit_bytes=40 * MIB
        ),
    )(
        tile_heads,
        tile_stream,
        stream_scale[None],
        final_gain[None],
        final_bias[None],
        embed_bias[None],
        slide_gain[None],
        head_weight,
        embed_weight,
        triple_weight,
    )
    tiles = pl.pallas_call(
        attention_kernel,
        out_shape=jax.ShapeDtypeStruct((HEADS, HEAD_DIM, TILE_DEV), BF16),
        in_specs=[smem, vmem],
        out_specs=vmem,
        scratch_shapes=[
            pltpu.VMEM((2 * HALF + slots, 128), F32),
            pltpu.VMEM((2 * HALF + slots, 128), F32),
        ],
        compiler_params=pltpu.CompilerParams(vmem_limit_bytes=40 * MIB),
    )(tissue_counts, pieces)
    return pl.pallas_call(
        project_kernel,
        out_shape=jax.ShapeDtypeStruct((TILE_DEV, output_weight.shape[1]), BF16),
        in_specs=[vmem] * 3,
        out_specs=vmem,
        scratch_shapes=[
            pltpu.VMEM((HEADS, HEAD_DIM, TILE_DEV), BF16),
            dma,
            dma((HEADS,)),
            dma((HEADS,)),
        ],
        compiler_params=pltpu.CompilerParams(
            collective_id=1, has_side_effects=True, vmem_limit_bytes=16 * MIB
        ),
    )(tiles, inner_gain[:, None], output_weight)


def solution(mesh):
    placed = (
        P(("groups", "seq"), None),
        P(("groups", "seq"), None),
        P("groups"),
        P(),
        P(),
        P(),
        P(),
        P(),
        P(),
        P(),
        P(),
        P(),
        P(),
    )
    return jax.shard_map(
        local, mesh=mesh, in_specs=placed, out_specs=P(("groups", "seq"), None), check_vma=False
    )
```

```python
import math

import jax
import jax.numpy as jnp
import numpy as np
from jax import lax
from jax.experimental import pallas as pl
from jax.experimental.pallas import tpu as pltpu
from jax.sharding import PartitionSpec as P

HEAD_DIM = 48
HEADS = 8
BRANCHES = 5
SEG_BASE = 1024
TILE_DEV = 128


EPSILON = 1e-06
NEGATIVE = -1e30


def swapped(block, axis, stride):
    count = lax.axis_size(axis)
    route = []
    for low in range(count):
        high = low | 1 << stride
        if high != low and high < count:
            route += [(low, high), (high, low)]
    return lax.ppermute(block, axis, route)


def layer_norm(values, gain_vector):
    average = jnp.mean(values, axis=-1, keepdims=True)
    centred = values - average
    spread = jnp.mean(centred * centred, axis=-1, keepdims=True)
    return centred * lax.rsqrt(spread + EPSILON) * gain_vector


def encode(head_rows, stream_rows, head_weight, stream_scale, final_gain, final_bias):
    blended = jnp.dot(head_rows, head_weight, preferred_element_type=jnp.float32)
    summed = stream_rows.astype(jnp.float32) + stream_scale * blended
    return (layer_norm(summed, final_gain) + final_bias).astype(jnp.bfloat16)


def project(embedding, embed_weight, embed_bias):
    return (
        jnp.dot(embedding, embed_weight, preferred_element_type=jnp.float32) + embed_bias
    ).astype(jnp.bfloat16)


def member_table(stride):
    return np.arange(stride)[:, None] == (np.arange(HEADS) % stride)[None, :]


def select_heads(source, stride):
    shaped = source.reshape(source.shape[0] // stride, stride, HEADS, source.shape[-1])
    member = member_table(stride)[None, :, :, None]
    return jnp.sum(jnp.where(member, shaped, jnp.zeros((), shaped.dtype)), axis=1)


def spread_heads(values, stride, fill_value):
    member = member_table(stride)
    if values.ndim == 3:
        member = member[:, :, None]
    member = member[None]
    placed = jnp.where(member, values[:, None], jnp.asarray(fill_value, values.dtype))
    return placed.reshape((values.shape[0] * stride,) + values.shape[1:])


def local_general(
    tile_heads,
    tile_stream,
    tissue_counts,
    head_weight,
    stream_scale,
    final_gain,
    final_bias,
    embed_weight,
    embed_bias,
    slide_gain,
    triple_weight,
    inner_gain,
    output_weight,
):
    devices = lax.axis_size("seq")
    rank_here = lax.axis_index("seq")
    capacity = tile_heads.shape[0] // devices
    per_peer = TILE_DEV // devices
    starts = jnp.cumsum(tissue_counts) - tissue_counts
    own_start = starts[rank_here]

    def outbound(source):
        shaped = source.reshape(capacity, devices, source.shape[-1])
        return jnp.roll(shaped, own_start % devices, axis=1)

    column = jnp.remainder(rank_here - starts, devices)
    slot_ids = jnp.arange(capacity, dtype=jnp.int32)[:, None] * devices + column[None, :]
    filled = slot_ids < tissue_counts[None, :]
    home_slot = (starts[None, :] + slot_ids) // devices
    target = jnp.where(filled, home_slot, TILE_DEV).reshape(capacity * devices)

    def place_rows(arrived):
        flattened = arrived.reshape(capacity * devices, arrived.shape[-1])
        return (
            jnp.zeros((TILE_DEV, flattened.shape[-1]), flattened.dtype)
            .at[target]
            .set(flattened, mode="drop")
        )

    head_in, stream_in = (
        lax.all_to_all(outbound(tile_heads), "seq", split_axis=1, concat_axis=1, tiled=True),
        lax.all_to_all(outbound(tile_stream), "seq", split_axis=1, concat_axis=1, tiled=True),
    )
    embedding = encode(
        place_rows(head_in),
        place_rows(stream_in),
        head_weight,
        stream_scale,
        final_gain,
        final_bias,
    )
    back_home = lax.all_to_all(
        embedding.reshape(devices, per_peer, 1, embedding.shape[-1]),
        "seq",
        split_axis=0,
        concat_axis=2,
        tiled=True,
    )
    slide_rows = project(back_home.reshape(TILE_DEV, embedding.shape[-1]), embed_weight, embed_bias)
    normed = layer_norm(slide_rows.astype(jnp.float32), slide_gain).astype(jnp.bfloat16)
    triple = jnp.dot(normed, triple_weight, preferred_element_type=jnp.float32).astype(jnp.bfloat16)
    inner_width = HEADS * HEAD_DIM
    queries = triple[:, :inner_width].reshape(TILE_DEV, HEADS, HEAD_DIM)
    key_value = jnp.concatenate(
        [
            triple[:, inner_width : 2 * inner_width].reshape(TILE_DEV, HEADS, HEAD_DIM),
            triple[:, 2 * inner_width :].reshape(TILE_DEV, HEADS, HEAD_DIM),
        ],
        axis=2,
    )
    total_rows = TILE_DEV * devices
    strides = [2**branch for branch in range(BRANCHES)]
    depths = [
        (min(SEG_BASE * stride, total_rows) // TILE_DEV).bit_length() - 1 for stride in strides
    ]
    blocks = [
        select_heads(key_value, stride).reshape(TILE_DEV // stride, 2 * inner_width)
        for stride in strides
    ]
    gathered = []
    for branch in range(BRANCHES):
        current = blocks[branch]
        for bit_place in range(depths[branch]):
            partner = swapped(current, "seq", bit_place)
            current = jnp.concatenate([current, partner], axis=0)
        gathered.append(current)
    scaling = 1.0 / math.sqrt(HEAD_DIM)
    high_list, total_list, mix_list = ([], [], [])
    for branch in range(BRANCHES):
        stride = strides[branch]
        own_queries = select_heads(queries, stride)
        gathered_rows = gathered[branch].reshape(-1, HEADS, 2 * HEAD_DIM)
        scores = (
            jnp.einsum(
                "qhd,khd->hqk",
                own_queries,
                gathered_rows[:, :, :HEAD_DIM],
                preferred_element_type=jnp.float32,
            )
            * scaling
        )
        highest = jnp.max(scores, axis=2)
        weights = jnp.exp(scores - highest[:, :, None])
        summed = jnp.sum(weights, axis=2)
        blended = jnp.einsum(
            "hqk,khd->qhd",
            weights.astype(jnp.bfloat16),
            gathered_rows[:, :, HEAD_DIM:],
            preferred_element_type=jnp.float32,
        )
        high_list.append(spread_heads(highest.T, stride, NEGATIVE))
        total_list.append(spread_heads(summed.T, stride, 0.0))
        mix_list.append(spread_heads(blended, stride, 0.0))
    high_all = jnp.stack(high_list)
    summit = jnp.max(high_all, axis=0)
    factor = jnp.exp(high_all - summit)
    denominator = jnp.sum(jnp.stack(total_list) * factor, axis=0)
    numerator = jnp.sum(jnp.stack(mix_list) * factor[..., None], axis=0)
    mixed = (numerator / denominator[..., None]).reshape(TILE_DEV, inner_width)
    inner = layer_norm(mixed, inner_gain).astype(jnp.bfloat16)
    return jnp.dot(inner, output_weight, preferred_element_type=jnp.float32).astype(jnp.bfloat16)


MESH = pl.DeviceIdType.MESH
PIECE = 3 * HEAD_DIM
HALF = 1024
NT = (((1,), (1,)), ((), ()))
TN = (((0,), (0,)), ((), ()))
F32 = jnp.float32
BF16 = jnp.bfloat16
MIB = 2**20


ROUTE = (4, 3, 5, 2, 6, 1, 7)
HALVES = 2


def encode_kernel(
    heads_hbm,
    stream_hbm,
    scale_ref,
    gain_ref,
    bias_ref,
    embed_bias_ref,
    slide_gain_ref,
    head_weight_hbm,
    embed_weight_hbm,
    triple_weight_hbm,
    recv_ref,
    heads,
    stream,
    head_weight,
    embed_weight,
    triple_weight,
    outbox,
    load_sem,
    own_sem,
    send_sem,
    pass_sem,
    recv_sem,
):
    group = lax.axis_index("groups")
    me = lax.axis_index("seq")
    chip, core = me // 2, lax.rem(me, 2)
    sibling = 2 * chip + 1 - core
    chips = HEADS
    depth = head_weight.shape[0]
    part = depth // 4
    rows = heads.shape[0] // HALVES

    def load(source, target, first, count, sem):
        copy = pltpu.make_async_copy(
            source.at[pl.ds(first, count)], target.at[pl.ds(first, count)], load_sem.at[sem]
        )
        copy.start()
        return copy

    head_loads = [load(heads_hbm, heads, 0, rows, 0)]
    weight_loads = [
        load(head_weight_hbm, head_weight, i * part, part, 1 + i) for i in range(4)
    ]
    stream_loads = [load(stream_hbm, stream, 0, rows, 5)]
    embed_load = load(embed_weight_hbm, embed_weight, 0, embed_weight.shape[0], 6)
    triple_load = load(triple_weight_hbm, triple_weight, 0, triple_weight.shape[0], 7)
    head_loads.append(load(heads_hbm, heads, rows, rows, 8))
    stream_loads.append(load(stream_hbm, stream, rows, rows, 9))

    barrier = pltpu.get_barrier_semaphore()
    for off in range(1, chips):
        peer = 2 * lax.rem(chip + off, chips) + core
        pl.semaphore_signal(barrier, inc=1, device_id=(group, peer), device_id_type=MESH)
    pl.semaphore_signal(barrier, inc=1, device_id=(group, sibling), device_id_type=MESH)

    inner = HEADS * HEAD_DIM
    scale = scale_ref[...].reshape(1, -1)
    gain = gain_ref[...].reshape(1, -1)
    bias = bias_ref[...].reshape(1, -1)
    embed_bias = embed_bias_ref[...].reshape(1, -1)
    slide_gain = slide_gain_ref[...].reshape(1, -1)
    sends = []
    owns = []
    for half in range(HALVES):
        low = half * rows
        head_loads[half].wait()
        blended = None
        for i in range(4):
            if half == 0:
                weight_loads[i].wait()
            term = jnp.dot(
                heads[low : low + rows, i * part : (i + 1) * part],
                head_weight[i * part : (i + 1) * part, :],
                preferred_element_type=F32,
            )
            blended = term if blended is None else blended + term
        stream_loads[half].wait()
        summed = stream[low : low + rows, :].astype(F32) + scale * blended
        embedding = (layer_norm(summed, gain) + bias).astype(BF16)
        if half == 0:
            embed_load.wait()
        slide_rows = (
            jnp.dot(embedding, embed_weight[...], preferred_element_type=F32) + embed_bias
        ).astype(BF16)
        normed = layer_norm(slide_rows.astype(F32), slide_gain).astype(BF16)
        if half == 0:
            triple_load.wait()
        triple = jnp.dot(normed, triple_weight[...], preferred_element_type=F32)
        turned = triple.T.astype(BF16)
        for h in range(HEADS):
            for kind in range(3):
                first = kind * inner + h * HEAD_DIM
                outbox[half, h, kind * HEAD_DIM : (kind + 1) * HEAD_DIM, :] = turned[
                    first : first + HEAD_DIM, :
                ]
        if half == 0:
            pl.semaphore_wait(barrier, chips)
        for off in ROUTE + (0,):
            to = lax.rem(chip + off, chips)
            copy = pltpu.make_async_remote_copy(
                src_ref=outbox.at[half, to],
                dst_ref=recv_ref.at[me, half],
                send_sem=send_sem.at[half, off],
                recv_sem=recv_sem.at[me, half],
                device_id=(group, 2 * to + core if off else sibling),
                device_id_type=MESH,
            )
            copy.start()
            sends.append(copy)
        own = pltpu.make_async_copy(
            outbox.at[half, chip], recv_ref.at[me, half], own_sem.at[half]
        )
        own.start()
        owns.append(own)

    def arrival(source, half, sem):
        return pltpu.make_async_remote_copy(
            src_ref=recv_ref.at[source, half],
            dst_ref=recv_ref.at[source, half],
            send_sem=sem,
            recv_sem=recv_sem.at[source, half],
            device_id=(group, sibling),
            device_id_type=MESH,
        )

    for half in range(HALVES):
        for off in ROUTE:
            source = 2 * lax.rem(chip + chips - off, chips) + core
            onward = arrival(source, half, pass_sem.at[half, off])
            onward.wait_recv()
            onward.start()
            sends.append(onward)
    for half in range(HALVES):
        for off in range(chips):
            source = 2 * lax.rem(chip + chips - off, chips) + 1 - core
            arrival(source, half, pass_sem.at[half, 0]).wait_recv()
    for copy in sends:
        copy.wait_send()
    for own in owns:
        own.wait()


def shared_depth(index, shift):
    residue = (index + 8 - shift) & 7
    depth = jnp.where(residue & 4 != 0, 3, 4)
    depth = jnp.where(residue & 2 != 0, 2, depth)
    return jnp.where(residue & 1 != 0, 1, depth)


def attend(keys, queries, multiplicity):
    scaling = 1.0 / math.sqrt(HEAD_DIM)
    scores = [
        lax.dot_general(block, queries, NT, preferred_element_type=F32) for block in keys
    ]
    highest = scores[0].max(axis=0, keepdims=True)
    for block in scores[1:]:
        highest = jnp.maximum(highest, block.max(axis=0, keepdims=True))
    total = blended = None
    for block, values, times in zip(scores, keys, multiplicity):
        weights = jnp.exp((block - highest) * scaling)
        if times is not None:
            weights = weights * times
        part_total = weights.sum(axis=0, keepdims=True)
        part = lax.dot_general(values, weights.astype(BF16), TN, preferred_element_type=F32)
        total = part_total if total is None else total + part_total
        blended = part if blended is None else blended + part
    return blended[2 * HEAD_DIM : PIECE, :] / total


def attention_kernel(counts_ref, pieces_ref, out_ref, left, right):
    me = lax.axis_index("seq")
    head, side = me // 2, lax.rem(me, 2)
    parity, shift = lax.rem(head, 2), head // 2
    slots = pieces_ref.shape[1] * pieces_ref.shape[3]
    unit = (
        lax.broadcasted_iota(jnp.int32, (slots, slots), 0)
        == lax.broadcasted_iota(jnp.int32, (slots, slots), 1)
    ).astype(BF16)
    right[...] = jnp.zeros_like(right)
    start = 0
    for d in range(pieces_ref.shape[0]):
        block = jnp.concatenate([pieces_ref[d, half] for half in range(HALVES)], axis=1)
        rows = lax.dot_general(unit, block, NT, preferred_element_type=F32)
        left[pl.ds(start, slots), :] = rows[:, :128]
        right[pl.ds(start, slots), : PIECE - 128] = rows[:, 128:]
        start = start + counts_ref[d]

    def pick(first, which):
        place = pl.ds(first + which, HALF // 2, stride=2)
        return jnp.concatenate(
            [left[place, :].astype(BF16), right[place, :].astype(BF16)], axis=1
        )

    def as_queries(rows):
        lane = lax.broadcasted_iota(jnp.int32, (HALF // 2, 128), 1)
        kept = jnp.where(lane < HEAD_DIM, rows[:, :128].astype(F32), 0.0)
        moved = pltpu.roll(kept, HEAD_DIM, 1).astype(BF16)
        return jnp.concatenate([moved, jnp.zeros_like(moved)], axis=1)

    near = pick(side * HALF, parity)
    near_off = pick(side * HALF, 1 - parity)
    far = pick((1 - side) * HALF, parity)
    count = HALF // 2
    key_depth = shared_depth(lax.broadcasted_iota(jnp.int32, (count, 1), 0), shift)
    query_depth = shared_depth(lax.broadcasted_iota(jnp.int32, (1, count), 1), shift)
    times = jnp.minimum(key_depth, query_depth).astype(F32)
    same = attend([near, near_off, far], as_queries(near), [times + 1.0, None, times])
    off = attend([near, near_off], as_queries(near_off), [None, None])
    even = jnp.where(parity == 0, same, off).astype(BF16)
    odd = jnp.where(parity == 0, off, same).astype(BF16)
    for t in range(HALF // TILE_DEV):
        low = t * (TILE_DEV // 2)
        out_ref[t] = jnp.concatenate(
            [even[:, low : low + TILE_DEV // 2], odd[:, low : low + TILE_DEV // 2]], axis=1
        )


def project_kernel(tiles_ref, gain_ref, weight_ref, out_ref, inbox, own_sem, send_sem, recv_sem):
    group = lax.axis_index("groups")
    me = lax.axis_index("seq")
    head, side = me // 2, lax.rem(me, 2)
    home_side = me // HEADS
    barrier = pltpu.get_barrier_semaphore()
    for h in range(HEADS):

        @pl.when(2 * h + home_side != me)
        def _():
            pl.semaphore_signal(
                barrier, inc=1, device_id=(group, 2 * h + home_side), device_id_type=MESH
            )

    pl.semaphore_wait(barrier, HEADS - jnp.where(side == home_side, 1, 0))

    def remote(t):
        return pltpu.make_async_remote_copy(
            src_ref=tiles_ref.at[t],
            dst_ref=inbox.at[head],
            send_sem=send_sem.at[t],
            recv_sem=recv_sem.at[head],
            device_id=(group, side * HEADS + t),
            device_id_type=MESH,
        )

    for t in range(HEADS):

        @pl.when(side * HEADS + t != me)
        def _():
            remote(t).start()

        @pl.when(side * HEADS + t == me)
        def _():
            own = pltpu.make_async_copy(tiles_ref.at[t], inbox.at[head], own_sem)
            own.start()
            own.wait()

    for h in range(HEADS):

        @pl.when(2 * h + home_side != me)
        def _():
            pltpu.make_async_remote_copy(
                src_ref=tiles_ref.at[0],
                dst_ref=inbox.at[h],
                send_sem=send_sem.at[0],
                recv_sem=recv_sem.at[h],
                device_id=(group, 2 * h + home_side),
                device_id_type=MESH,
            ).wait_recv()

    mixed = inbox[...].astype(F32).reshape(HEADS * HEAD_DIM, TILE_DEV)
    average = jnp.mean(mixed, axis=0, keepdims=True)
    centred = mixed - average
    spread = jnp.mean(centred * centred, axis=0, keepdims=True)
    inner = (centred * lax.rsqrt(spread + EPSILON) * gain_ref[...]).astype(BF16)
    row = lax.broadcasted_iota(jnp.int32, (TILE_DEV, TILE_DEV), 0)
    lane = lax.broadcasted_iota(jnp.int32, (TILE_DEV, TILE_DEV), 1)
    half = TILE_DEV // 2
    order = (row == 2 * lax.rem(lane, half) + lane // half).astype(BF16)
    rows = lax.dot_general(order, inner, NT, preferred_element_type=F32).astype(BF16)
    out_ref[...] = jnp.dot(rows, weight_ref[...], preferred_element_type=F32).astype(BF16)
    for t in range(HEADS):

        @pl.when(side * HEADS + t != me)
        def _():
            remote(t).wait_send()


def local(
    tile_heads,
    tile_stream,
    tissue_counts,
    head_weight,
    stream_scale,
    final_gain,
    final_bias,
    embed_weight,
    embed_bias,
    slide_gain,
    triple_weight,
    inner_gain,
    output_weight,
):
    devices = lax.axis_size("seq")
    if devices != 2 * HEADS:
        return local_general(
            tile_heads,
            tile_stream,
            tissue_counts,
            head_weight,
            stream_scale,
            final_gain,
            final_bias,
            embed_weight,
            embed_bias,
            slide_gain,
            triple_weight,
            inner_gain,
            output_weight,
        )
    slots = tile_heads.shape[0]
    vmem = pl.BlockSpec(memory_space=pltpu.VMEM)
    smem = pl.BlockSpec(memory_space=pltpu.SMEM)
    hbm = pl.BlockSpec(memory_space=pl.ANY)
    dma = pltpu.SemaphoreType.DMA
    pieces = pl.pallas_call(
        encode_kernel,
        out_shape=jax.ShapeDtypeStruct((devices, HALVES, PIECE, slots // HALVES), BF16),
        in_specs=[hbm] * 2 + [vmem] * 5 + [hbm] * 3,
        out_specs=vmem,
        scratch_shapes=[
            pltpu.VMEM(tile_heads.shape, BF16),
            pltpu.VMEM(tile_stream.shape, BF16),
            pltpu.VMEM(head_weight.shape, BF16),
            pltpu.VMEM(embed_weight.shape, BF16),
            pltpu.VMEM(triple_weight.shape, BF16),
            pltpu.VMEM((HALVES, HEADS, PIECE, slots // HALVES), BF16),
            dma((10,)),
            dma((HALVES,)),
            dma((HALVES, HEADS)),
            dma((HALVES, HEADS)),
            dma((devices, HALVES)),
        ],
        compiler_params=pltpu.CompilerParams(
            collective_id=0, has_side_effects=True, vmem_limit_bytes=56 * MIB
        ),
    )(
        tile_heads,
        tile_stream,
        stream_scale,
        final_gain,
        final_bias,
        embed_bias,
        slide_gain,
        head_weight,
        embed_weight,
        triple_weight,
    )
    tiles = pl.pallas_call(
        attention_kernel,
        out_shape=jax.ShapeDtypeStruct((HEADS, HEAD_DIM, TILE_DEV), BF16),
        in_specs=[smem, vmem],
        out_specs=vmem,
        scratch_shapes=[
            pltpu.VMEM((2 * HALF + slots, 128), F32),
            pltpu.VMEM((2 * HALF + slots, 128), F32),
        ],
        compiler_params=pltpu.CompilerParams(vmem_limit_bytes=40 * MIB),
    )(tissue_counts, pieces)
    return pl.pallas_call(
        project_kernel,
        out_shape=jax.ShapeDtypeStruct((TILE_DEV, output_weight.shape[1]), BF16),
        in_specs=[vmem] * 3,
        out_specs=vmem,
        scratch_shapes=[
            pltpu.VMEM((HEADS, HEAD_DIM, TILE_DEV), BF16),
            dma,
            dma((HEADS,)),
            dma((HEADS,)),
        ],
        compiler_params=pltpu.CompilerParams(
            collective_id=1, has_side_effects=True, vmem_limit_bytes=16 * MIB
        ),
    )(tiles, inner_gain[:, None], output_weight)


def solution(mesh):
    placed = (
        P(("groups", "seq"), None),
        P(("groups", "seq"), None),
        P("groups"),
        P(),
        P(),
        P(),
        P(),
        P(),
        P(),
        P(),
        P(),
        P(),
        P(),
    )
    return jax.shard_map(
        local, mesh=mesh, in_specs=placed, out_specs=P(("groups", "seq"), None), check_vma=False
    )
```

```python
import math

import jax
import jax.numpy as jnp
import numpy as np
from jax import lax
from jax.experimental import pallas as pl
from jax.experimental.pallas import tpu as pltpu
from jax.sharding import PartitionSpec as P

HEAD_DIM = 48
HEADS = 8
BRANCHES = 5
SEG_BASE = 1024
TILE_DEV = 128


EPSILON = 1e-06
NEGATIVE = -1e30


def swapped(block, axis, stride):
    count = lax.axis_size(axis)
    route = []
    for low in range(count):
        high = low | 1 << stride
        if high != low and high < count:
            route += [(low, high), (high, low)]
    return lax.ppermute(block, axis, route)


def layer_norm(values, gain_vector):
    average = jnp.mean(values, axis=-1, keepdims=True)
    centred = values - average
    spread = jnp.mean(centred * centred, axis=-1, keepdims=True)
    return centred * lax.rsqrt(spread + EPSILON) * gain_vector


def encode(head_rows, stream_rows, head_weight, stream_scale, final_gain, final_bias):
    blended = jnp.dot(head_rows, head_weight, preferred_element_type=jnp.float32)
    summed = stream_rows.astype(jnp.float32) + stream_scale * blended
    return (layer_norm(summed, final_gain) + final_bias).astype(jnp.bfloat16)


def project(embedding, embed_weight, embed_bias):
    return (
        jnp.dot(embedding, embed_weight, preferred_element_type=jnp.float32) + embed_bias
    ).astype(jnp.bfloat16)


def member_table(stride):
    return np.arange(stride)[:, None] == (np.arange(HEADS) % stride)[None, :]


def select_heads(source, stride):
    shaped = source.reshape(source.shape[0] // stride, stride, HEADS, source.shape[-1])
    member = member_table(stride)[None, :, :, None]
    return jnp.sum(jnp.where(member, shaped, jnp.zeros((), shaped.dtype)), axis=1)


def spread_heads(values, stride, fill_value):
    member = member_table(stride)
    if values.ndim == 3:
        member = member[:, :, None]
    member = member[None]
    placed = jnp.where(member, values[:, None], jnp.asarray(fill_value, values.dtype))
    return placed.reshape((values.shape[0] * stride,) + values.shape[1:])


def local_general(
    tile_heads,
    tile_stream,
    tissue_counts,
    head_weight,
    stream_scale,
    final_gain,
    final_bias,
    embed_weight,
    embed_bias,
    slide_gain,
    triple_weight,
    inner_gain,
    output_weight,
):
    devices = lax.axis_size("seq")
    rank_here = lax.axis_index("seq")
    capacity = tile_heads.shape[0] // devices
    per_peer = TILE_DEV // devices
    starts = jnp.cumsum(tissue_counts) - tissue_counts
    own_start = starts[rank_here]

    def outbound(source):
        shaped = source.reshape(capacity, devices, source.shape[-1])
        return jnp.roll(shaped, own_start % devices, axis=1)

    column = jnp.remainder(rank_here - starts, devices)
    slot_ids = jnp.arange(capacity, dtype=jnp.int32)[:, None] * devices + column[None, :]
    filled = slot_ids < tissue_counts[None, :]
    home_slot = (starts[None, :] + slot_ids) // devices
    target = jnp.where(filled, home_slot, TILE_DEV).reshape(capacity * devices)

    def place_rows(arrived):
        flattened = arrived.reshape(capacity * devices, arrived.shape[-1])
        return (
            jnp.zeros((TILE_DEV, flattened.shape[-1]), flattened.dtype)
            .at[target]
            .set(flattened, mode="drop")
        )

    head_in, stream_in = (
        lax.all_to_all(outbound(tile_heads), "seq", split_axis=1, concat_axis=1, tiled=True),
        lax.all_to_all(outbound(tile_stream), "seq", split_axis=1, concat_axis=1, tiled=True),
    )
    embedding = encode(
        place_rows(head_in),
        place_rows(stream_in),
        head_weight,
        stream_scale,
        final_gain,
        final_bias,
    )
    back_home = lax.all_to_all(
        embedding.reshape(devices, per_peer, 1, embedding.shape[-1]),
        "seq",
        split_axis=0,
        concat_axis=2,
        tiled=True,
    )
    slide_rows = project(back_home.reshape(TILE_DEV, embedding.shape[-1]), embed_weight, embed_bias)
    normed = layer_norm(slide_rows.astype(jnp.float32), slide_gain).astype(jnp.bfloat16)
    triple = jnp.dot(normed, triple_weight, preferred_element_type=jnp.float32).astype(jnp.bfloat16)
    inner_width = HEADS * HEAD_DIM
    queries = triple[:, :inner_width].reshape(TILE_DEV, HEADS, HEAD_DIM)
    key_value = jnp.concatenate(
        [
            triple[:, inner_width : 2 * inner_width].reshape(TILE_DEV, HEADS, HEAD_DIM),
            triple[:, 2 * inner_width :].reshape(TILE_DEV, HEADS, HEAD_DIM),
        ],
        axis=2,
    )
    total_rows = TILE_DEV * devices
    strides = [2**branch for branch in range(BRANCHES)]
    depths = [
        (min(SEG_BASE * stride, total_rows) // TILE_DEV).bit_length() - 1 for stride in strides
    ]
    blocks = [
        select_heads(key_value, stride).reshape(TILE_DEV // stride, 2 * inner_width)
        for stride in strides
    ]
    gathered = []
    for branch in range(BRANCHES):
        current = blocks[branch]
        for bit_place in range(depths[branch]):
            partner = swapped(current, "seq", bit_place)
            current = jnp.concatenate([current, partner], axis=0)
        gathered.append(current)
    scaling = 1.0 / math.sqrt(HEAD_DIM)
    high_list, total_list, mix_list = ([], [], [])
    for branch in range(BRANCHES):
        stride = strides[branch]
        own_queries = select_heads(queries, stride)
        gathered_rows = gathered[branch].reshape(-1, HEADS, 2 * HEAD_DIM)
        scores = (
            jnp.einsum(
                "qhd,khd->hqk",
                own_queries,
                gathered_rows[:, :, :HEAD_DIM],
                preferred_element_type=jnp.float32,
            )
            * scaling
        )
        highest = jnp.max(scores, axis=2)
        weights = jnp.exp(scores - highest[:, :, None])
        summed = jnp.sum(weights, axis=2)
        blended = jnp.einsum(
            "hqk,khd->qhd",
            weights.astype(jnp.bfloat16),
            gathered_rows[:, :, HEAD_DIM:],
            preferred_element_type=jnp.float32,
        )
        high_list.append(spread_heads(highest.T, stride, NEGATIVE))
        total_list.append(spread_heads(summed.T, stride, 0.0))
        mix_list.append(spread_heads(blended, stride, 0.0))
    high_all = jnp.stack(high_list)
    summit = jnp.max(high_all, axis=0)
    factor = jnp.exp(high_all - summit)
    denominator = jnp.sum(jnp.stack(total_list) * factor, axis=0)
    numerator = jnp.sum(jnp.stack(mix_list) * factor[..., None], axis=0)
    mixed = (numerator / denominator[..., None]).reshape(TILE_DEV, inner_width)
    inner = layer_norm(mixed, inner_gain).astype(jnp.bfloat16)
    return jnp.dot(inner, output_weight, preferred_element_type=jnp.float32).astype(jnp.bfloat16)


MESH = pl.DeviceIdType.MESH
PIECE = 3 * HEAD_DIM
HALF = 1024
NT = (((1,), (1,)), ((), ()))
TN = (((0,), (0,)), ((), ()))
F32 = jnp.float32
BF16 = jnp.bfloat16
MIB = 2**20


ROUTE = (4, 3, 5, 2, 6, 1, 7)
HALVES = 2


def encode_kernel(
    heads_hbm,
    stream_hbm,
    scale_ref,
    gain_ref,
    bias_ref,
    embed_bias_ref,
    slide_gain_ref,
    head_weight_hbm,
    embed_weight_hbm,
    triple_weight_hbm,
    recv_ref,
    heads,
    stream,
    head_weight,
    embed_weight,
    triple_weight,
    outbox,
    load_sem,
    own_sem,
    send_sem,
    pass_sem,
    recv_sem,
):
    group = lax.axis_index("groups")
    me = lax.axis_index("seq")
    chip, core = me // 2, lax.rem(me, 2)
    sibling = 2 * chip + 1 - core
    chips = HEADS
    depth = head_weight.shape[0]
    part = depth // 4
    rows = heads.shape[0] // HALVES

    def load(source, target, first, count, sem):
        copy = pltpu.make_async_copy(
            source.at[pl.ds(first, count)], target.at[pl.ds(first, count)], load_sem.at[sem]
        )
        copy.start()
        return copy

    head_loads = [load(heads_hbm, heads, 0, rows, 0)]
    weight_loads = [
        load(head_weight_hbm, head_weight, i * part, part, 1 + i) for i in range(4)
    ]
    stream_loads = [load(stream_hbm, stream, 0, rows, 5)]
    embed_load = load(embed_weight_hbm, embed_weight, 0, embed_weight.shape[0], 6)
    triple_load = load(triple_weight_hbm, triple_weight, 0, triple_weight.shape[0], 7)
    head_loads.append(load(heads_hbm, heads, rows, rows, 8))
    stream_loads.append(load(stream_hbm, stream, rows, rows, 9))

    barrier = pltpu.get_barrier_semaphore()
    for off in range(1, chips):
        peer = 2 * lax.rem(chip + off, chips) + core
        pl.semaphore_signal(barrier, inc=1, device_id=(group, peer), device_id_type=MESH)
    pl.semaphore_signal(barrier, inc=1, device_id=(group, sibling), device_id_type=MESH)

    inner = HEADS * HEAD_DIM
    scale = scale_ref[...].reshape(1, -1)
    gain = gain_ref[...].reshape(1, -1)
    bias = bias_ref[...].reshape(1, -1)
    embed_bias = embed_bias_ref[...].reshape(1, -1)
    slide_gain = slide_gain_ref[...].reshape(1, -1)
    sends = []
    owns = []
    for half in range(HALVES):
        low = half * rows
        head_loads[half].wait()
        blended = None
        for i in range(4):
            if half == 0:
                weight_loads[i].wait()
            term = jnp.dot(
                heads[low : low + rows, i * part : (i + 1) * part],
                head_weight[i * part : (i + 1) * part, :],
                preferred_element_type=F32,
            )
            blended = term if blended is None else blended + term
        stream_loads[half].wait()
        summed = stream[low : low + rows, :].astype(F32) + scale * blended
        embedding = (layer_norm(summed, gain) + bias).astype(BF16)
        if half == 0:
            embed_load.wait()
        slide_rows = (
            jnp.dot(embedding, embed_weight[...], preferred_element_type=F32) + embed_bias
        ).astype(BF16)
        normed = layer_norm(slide_rows.astype(F32), slide_gain).astype(BF16)
        if half == 0:
            triple_load.wait()
        triple = jnp.dot(normed, triple_weight[...], preferred_element_type=F32)
        turned = triple.T.astype(BF16)
        for h in range(HEADS):
            for kind in range(3):
                first = kind * inner + h * HEAD_DIM
                outbox[half, h, kind * HEAD_DIM : (kind + 1) * HEAD_DIM, :] = turned[
                    first : first + HEAD_DIM, :
                ]
        if half == 0:
            pl.semaphore_wait(barrier, chips)
        for off in ROUTE + (0,):
            to = lax.rem(chip + off, chips)
            copy = pltpu.make_async_remote_copy(
                src_ref=outbox.at[half, to],
                dst_ref=recv_ref.at[me, half],
                send_sem=send_sem.at[half, off],
                recv_sem=recv_sem.at[me, half],
                device_id=(group, 2 * to + core if off else sibling),
                device_id_type=MESH,
            )
            copy.start()
            sends.append(copy)
        own = pltpu.make_async_copy(
            outbox.at[half, chip], recv_ref.at[me, half], own_sem.at[half]
        )
        own.start()
        owns.append(own)

    def arrival(source, half, sem):
        return pltpu.make_async_remote_copy(
            src_ref=recv_ref.at[source, half],
            dst_ref=recv_ref.at[source, half],
            send_sem=sem,
            recv_sem=recv_sem.at[source, half],
            device_id=(group, sibling),
            device_id_type=MESH,
        )

    for half in range(HALVES):
        for off in ROUTE:
            source = 2 * lax.rem(chip + chips - off, chips) + core
            onward = arrival(source, half, pass_sem.at[half, off])
            onward.wait_recv()
            onward.start()
            sends.append(onward)
    for half in range(HALVES):
        for off in range(chips):
            source = 2 * lax.rem(chip + chips - off, chips) + 1 - core
            arrival(source, half, pass_sem.at[half, 0]).wait_recv()
    for copy in sends:
        copy.wait_send()
    for own in owns:
        own.wait()


def shared_depth(index, shift):
    residue = (index + 8 - shift) & 7
    depth = jnp.where(residue & 4 != 0, 3, 4)
    depth = jnp.where(residue & 2 != 0, 2, depth)
    return jnp.where(residue & 1 != 0, 1, depth)


def attend(keys, queries, multiplicity):
    scaling = 1.0 / math.sqrt(HEAD_DIM)
    scores = [
        lax.dot_general(block, queries, NT, preferred_element_type=F32) for block in keys
    ]
    highest = scores[0].max(axis=0, keepdims=True)
    for block in scores[1:]:
        highest = jnp.maximum(highest, block.max(axis=0, keepdims=True))
    total = blended = None
    for block, values, times in zip(scores, keys, multiplicity):
        weights = jnp.exp((block - highest) * scaling)
        if times is not None:
            weights = weights * times
        part_total = weights.sum(axis=0, keepdims=True)
        part = lax.dot_general(values, weights.astype(BF16), TN, preferred_element_type=F32)
        total = part_total if total is None else total + part_total
        blended = part if blended is None else blended + part
    return blended[2 * HEAD_DIM : PIECE, :] / total


def compact_kernel(counts_ref, pieces, near_ref, off_ref, far_ref, left, right):
    me = lax.axis_index("seq")
    head, side = me // 2, lax.rem(me, 2)
    parity = lax.rem(head, 2)
    slots = pieces.shape[1] * pieces.shape[3]
    unit = (
        lax.broadcasted_iota(jnp.int32, (slots, slots), 0)
        == lax.broadcasted_iota(jnp.int32, (slots, slots), 1)
    ).astype(BF16)
    right[...] = jnp.zeros_like(right)
    start = 0
    for d in range(pieces.shape[0]):
        block = jnp.concatenate([pieces[d, half] for half in range(HALVES)], axis=1)
        rows = lax.dot_general(unit, block, NT, preferred_element_type=F32)
        left[pl.ds(start, slots), :] = rows[:, :128]
        right[pl.ds(start, slots), : PIECE - 128] = rows[:, 128:]
        start = start + counts_ref[d]

    def pick(target, first, which):
        place = pl.ds(first + which, HALF // 2, stride=2)
        target[:, :128] = left[place, :].astype(BF16)
        target[:, 128:] = right[place, :].astype(BF16)

    pick(near_ref, side * HALF, parity)
    pick(off_ref, side * HALF, 1 - parity)
    pick(far_ref, (1 - side) * HALF, parity)


def as_queries(rows):
    lane = lax.broadcasted_iota(jnp.int32, (HALF // 2, 128), 1)
    kept = jnp.where(lane < HEAD_DIM, rows[:, :128].astype(F32), 0.0)
    moved = pltpu.roll(kept, HEAD_DIM, 1).astype(BF16)
    return jnp.concatenate([moved, jnp.zeros_like(moved)], axis=1)


def attention_kernel(
    near_ref,
    off_ref,
    far_ref,
    gain_ref,
    weight_ref,
    out_ref,
    tiles_ref,
    inbox,
    own_sem,
    send_sem,
    recv_sem,
):
    group = lax.axis_index("groups")
    me = lax.axis_index("seq")
    head, side = me // 2, lax.rem(me, 2)
    parity, shift = lax.rem(head, 2), head // 2
    home_side = me // HEADS
    barrier = pltpu.get_barrier_semaphore()
    for h in range(HEADS):

        @pl.when(2 * h + home_side != me)
        def _():
            pl.semaphore_signal(
                barrier, inc=1, device_id=(group, 2 * h + home_side), device_id_type=MESH
            )

    near, near_off, far = near_ref[...], off_ref[...], far_ref[...]
    count = HALF // 2
    key_depth = shared_depth(lax.broadcasted_iota(jnp.int32, (count, 1), 0), shift)
    query_depth = shared_depth(lax.broadcasted_iota(jnp.int32, (1, count), 1), shift)
    times = jnp.minimum(key_depth, query_depth).astype(F32)
    same = attend([near, near_off, far], as_queries(near), [times + 1.0, None, times])
    off = attend([near, near_off], as_queries(near_off), [None, None])
    even = jnp.where(parity == 0, same, off).astype(BF16)
    odd = jnp.where(parity == 0, off, same).astype(BF16)
    for t in range(HALF // TILE_DEV):
        low = t * (TILE_DEV // 2)
        tiles_ref[t] = jnp.concatenate(
            [even[:, low : low + TILE_DEV // 2], odd[:, low : low + TILE_DEV // 2]], axis=1
        )
    pl.semaphore_wait(barrier, HEADS - jnp.where(side == home_side, 1, 0))

    def remote(t):
        return pltpu.make_async_remote_copy(
            src_ref=tiles_ref.at[t],
            dst_ref=inbox.at[head],
            send_sem=send_sem.at[t],
            recv_sem=recv_sem.at[head],
            device_id=(group, side * HEADS + t),
            device_id_type=MESH,
        )

    for t in range(HEADS):

        @pl.when(side * HEADS + t != me)
        def _():
            remote(t).start()

        @pl.when(side * HEADS + t == me)
        def _():
            own = pltpu.make_async_copy(tiles_ref.at[t], inbox.at[head], own_sem)
            own.start()
            own.wait()

    for h in range(HEADS):

        @pl.when(2 * h + home_side != me)
        def _():
            pltpu.make_async_remote_copy(
                src_ref=tiles_ref.at[0],
                dst_ref=inbox.at[h],
                send_sem=send_sem.at[0],
                recv_sem=recv_sem.at[h],
                device_id=(group, 2 * h + home_side),
                device_id_type=MESH,
            ).wait_recv()

    mixed = inbox[...].astype(F32).reshape(HEADS * HEAD_DIM, TILE_DEV)
    average = jnp.mean(mixed, axis=0, keepdims=True)
    centred = mixed - average
    spread = jnp.mean(centred * centred, axis=0, keepdims=True)
    inner = (centred * lax.rsqrt(spread + EPSILON) * gain_ref[...]).astype(BF16)
    row = lax.broadcasted_iota(jnp.int32, (TILE_DEV, TILE_DEV), 0)
    lane = lax.broadcasted_iota(jnp.int32, (TILE_DEV, TILE_DEV), 1)
    half = TILE_DEV // 2
    order = (row == 2 * lax.rem(lane, half) + lane // half).astype(BF16)
    rows = lax.dot_general(order, inner, NT, preferred_element_type=F32).astype(BF16)
    out_ref[...] = jnp.dot(rows, weight_ref[...], preferred_element_type=F32).astype(BF16)
    for t in range(HEADS):

        @pl.when(side * HEADS + t != me)
        def _():
            remote(t).wait_send()


def local(
    tile_heads,
    tile_stream,
    tissue_counts,
    head_weight,
    stream_scale,
    final_gain,
    final_bias,
    embed_weight,
    embed_bias,
    slide_gain,
    triple_weight,
    inner_gain,
    output_weight,
):
    devices = lax.axis_size("seq")
    if devices != 2 * HEADS:
        return local_general(
            tile_heads,
            tile_stream,
            tissue_counts,
            head_weight,
            stream_scale,
            final_gain,
            final_bias,
            embed_weight,
            embed_bias,
            slide_gain,
            triple_weight,
            inner_gain,
            output_weight,
        )
    slots = tile_heads.shape[0]
    vmem = pl.BlockSpec(memory_space=pltpu.VMEM)
    smem = pl.BlockSpec(memory_space=pltpu.SMEM)
    hbm = pl.BlockSpec(memory_space=pltpu.HBM)
    anywhere = pl.BlockSpec(memory_space=pl.ANY)
    dma = pltpu.SemaphoreType.DMA
    pieces = pl.pallas_call(
        encode_kernel,
        out_shape=jax.ShapeDtypeStruct((devices, HALVES, PIECE, slots // HALVES), BF16),
        in_specs=[hbm] * 2 + [vmem] * 5 + [hbm] * 3,
        out_specs=anywhere,
        scratch_shapes=[
            pltpu.VMEM(tile_heads.shape, BF16),
            pltpu.VMEM(tile_stream.shape, BF16),
            pltpu.VMEM(head_weight.shape, BF16),
            pltpu.VMEM(embed_weight.shape, BF16),
            pltpu.VMEM(triple_weight.shape, BF16),
            pltpu.VMEM((HALVES, HEADS, PIECE, slots // HALVES), BF16),
            dma((10,)),
            dma((HALVES,)),
            dma((HALVES, HEADS)),
            dma((HALVES, HEADS)),
            dma((devices, HALVES)),
        ],
        compiler_params=pltpu.CompilerParams(
            collective_id=0, has_side_effects=True, vmem_limit_bytes=56 * MIB
        ),
    )(
        tile_heads,
        tile_stream,
        stream_scale,
        final_gain,
        final_bias,
        embed_bias,
        slide_gain,
        head_weight,
        embed_weight,
        triple_weight,
    )
    listed = jax.ShapeDtypeStruct((HALF // 2, 256), BF16)
    near, off, far = pl.pallas_call(
        compact_kernel,
        out_shape=(listed, listed, listed),
        in_specs=[smem, vmem],
        out_specs=(vmem, vmem, vmem),
        scratch_shapes=[
            pltpu.VMEM((2 * HALF + slots, 128), F32),
            pltpu.VMEM((2 * HALF + slots, 128), F32),
        ],
        compiler_params=pltpu.CompilerParams(vmem_limit_bytes=24 * MIB),
    )(tissue_counts, pieces)
    return pl.pallas_call(
        attention_kernel,
        out_shape=jax.ShapeDtypeStruct((TILE_DEV, output_weight.shape[1]), BF16),
        in_specs=[vmem] * 5,
        out_specs=vmem,
        scratch_shapes=[
            pltpu.VMEM((HEADS, HEAD_DIM, TILE_DEV), BF16),
            pltpu.VMEM((HEADS, HEAD_DIM, TILE_DEV), BF16),
            dma,
            dma((HEADS,)),
            dma((HEADS,)),
        ],
        compiler_params=pltpu.CompilerParams(
            collective_id=1, has_side_effects=True, vmem_limit_bytes=32 * MIB
        ),
    )(near, off, far, inner_gain[:, None], output_weight)


def solution(mesh):
    placed = (
        P(("groups", "seq"), None),
        P(("groups", "seq"), None),
        P("groups"),
        P(),
        P(),
        P(),
        P(),
        P(),
        P(),
        P(),
        P(),
        P(),
        P(),
    )
    return jax.shard_map(
        local, mesh=mesh, in_specs=placed, out_specs=P(("groups", "seq"), None), check_vma=False
    )
```

```python
import math

import jax
import jax.numpy as jnp
import numpy as np
from jax import lax
from jax.experimental import pallas as pl
from jax.experimental.pallas import tpu as pltpu
from jax.sharding import PartitionSpec as P

HEAD_DIM = 48
HEADS = 8
BRANCHES = 5
SEG_BASE = 1024
TILE_DEV = 128


EPSILON = 1e-06
NEGATIVE = -1e30


def swapped(block, axis, stride):
    count = lax.axis_size(axis)
    route = []
    for low in range(count):
        high = low | 1 << stride
        if high != low and high < count:
            route += [(low, high), (high, low)]
    return lax.ppermute(block, axis, route)


def layer_norm(values, gain_vector):
    average = jnp.mean(values, axis=-1, keepdims=True)
    centred = values - average
    spread = jnp.mean(centred * centred, axis=-1, keepdims=True)
    return centred * lax.rsqrt(spread + EPSILON) * gain_vector


def encode(head_rows, stream_rows, head_weight, stream_scale, final_gain, final_bias):
    blended = jnp.dot(head_rows, head_weight, preferred_element_type=jnp.float32)
    summed = stream_rows.astype(jnp.float32) + stream_scale * blended
    return (layer_norm(summed, final_gain) + final_bias).astype(jnp.bfloat16)


def project(embedding, embed_weight, embed_bias):
    return (
        jnp.dot(embedding, embed_weight, preferred_element_type=jnp.float32) + embed_bias
    ).astype(jnp.bfloat16)


def member_table(stride):
    return np.arange(stride)[:, None] == (np.arange(HEADS) % stride)[None, :]


def select_heads(source, stride):
    shaped = source.reshape(source.shape[0] // stride, stride, HEADS, source.shape[-1])
    member = member_table(stride)[None, :, :, None]
    return jnp.sum(jnp.where(member, shaped, jnp.zeros((), shaped.dtype)), axis=1)


def spread_heads(values, stride, fill_value):
    member = member_table(stride)
    if values.ndim == 3:
        member = member[:, :, None]
    member = member[None]
    placed = jnp.where(member, values[:, None], jnp.asarray(fill_value, values.dtype))
    return placed.reshape((values.shape[0] * stride,) + values.shape[1:])


def local_general(
    tile_heads,
    tile_stream,
    tissue_counts,
    head_weight,
    stream_scale,
    final_gain,
    final_bias,
    embed_weight,
    embed_bias,
    slide_gain,
    triple_weight,
    inner_gain,
    output_weight,
):
    devices = lax.axis_size("seq")
    rank_here = lax.axis_index("seq")
    capacity = tile_heads.shape[0] // devices
    per_peer = TILE_DEV // devices
    starts = jnp.cumsum(tissue_counts) - tissue_counts
    own_start = starts[rank_here]

    def outbound(source):
        shaped = source.reshape(capacity, devices, source.shape[-1])
        return jnp.roll(shaped, own_start % devices, axis=1)

    column = jnp.remainder(rank_here - starts, devices)
    slot_ids = jnp.arange(capacity, dtype=jnp.int32)[:, None] * devices + column[None, :]
    filled = slot_ids < tissue_counts[None, :]
    home_slot = (starts[None, :] + slot_ids) // devices
    target = jnp.where(filled, home_slot, TILE_DEV).reshape(capacity * devices)

    def place_rows(arrived):
        flattened = arrived.reshape(capacity * devices, arrived.shape[-1])
        return (
            jnp.zeros((TILE_DEV, flattened.shape[-1]), flattened.dtype)
            .at[target]
            .set(flattened, mode="drop")
        )

    head_in, stream_in = (
        lax.all_to_all(outbound(tile_heads), "seq", split_axis=1, concat_axis=1, tiled=True),
        lax.all_to_all(outbound(tile_stream), "seq", split_axis=1, concat_axis=1, tiled=True),
    )
    embedding = encode(
        place_rows(head_in),
        place_rows(stream_in),
        head_weight,
        stream_scale,
        final_gain,
        final_bias,
    )
    back_home = lax.all_to_all(
        embedding.reshape(devices, per_peer, 1, embedding.shape[-1]),
        "seq",
        split_axis=0,
        concat_axis=2,
        tiled=True,
    )
    slide_rows = project(back_home.reshape(TILE_DEV, embedding.shape[-1]), embed_weight, embed_bias)
    normed = layer_norm(slide_rows.astype(jnp.float32), slide_gain).astype(jnp.bfloat16)
    triple = jnp.dot(normed, triple_weight, preferred_element_type=jnp.float32).astype(jnp.bfloat16)
    inner_width = HEADS * HEAD_DIM
    queries = triple[:, :inner_width].reshape(TILE_DEV, HEADS, HEAD_DIM)
    key_value = jnp.concatenate(
        [
            triple[:, inner_width : 2 * inner_width].reshape(TILE_DEV, HEADS, HEAD_DIM),
            triple[:, 2 * inner_width :].reshape(TILE_DEV, HEADS, HEAD_DIM),
        ],
        axis=2,
    )
    total_rows = TILE_DEV * devices
    strides = [2**branch for branch in range(BRANCHES)]
    depths = [
        (min(SEG_BASE * stride, total_rows) // TILE_DEV).bit_length() - 1 for stride in strides
    ]
    blocks = [
        select_heads(key_value, stride).reshape(TILE_DEV // stride, 2 * inner_width)
        for stride in strides
    ]
    gathered = []
    for branch in range(BRANCHES):
        current = blocks[branch]
        for bit_place in range(depths[branch]):
            partner = swapped(current, "seq", bit_place)
            current = jnp.concatenate([current, partner], axis=0)
        gathered.append(current)
    scaling = 1.0 / math.sqrt(HEAD_DIM)
    high_list, total_list, mix_list = ([], [], [])
    for branch in range(BRANCHES):
        stride = strides[branch]
        own_queries = select_heads(queries, stride)
        gathered_rows = gathered[branch].reshape(-1, HEADS, 2 * HEAD_DIM)
        scores = (
            jnp.einsum(
                "qhd,khd->hqk",
                own_queries,
                gathered_rows[:, :, :HEAD_DIM],
                preferred_element_type=jnp.float32,
            )
            * scaling
        )
        highest = jnp.max(scores, axis=2)
        weights = jnp.exp(scores - highest[:, :, None])
        summed = jnp.sum(weights, axis=2)
        blended = jnp.einsum(
            "hqk,khd->qhd",
            weights.astype(jnp.bfloat16),
            gathered_rows[:, :, HEAD_DIM:],
            preferred_element_type=jnp.float32,
        )
        high_list.append(spread_heads(highest.T, stride, NEGATIVE))
        total_list.append(spread_heads(summed.T, stride, 0.0))
        mix_list.append(spread_heads(blended, stride, 0.0))
    high_all = jnp.stack(high_list)
    summit = jnp.max(high_all, axis=0)
    factor = jnp.exp(high_all - summit)
    denominator = jnp.sum(jnp.stack(total_list) * factor, axis=0)
    numerator = jnp.sum(jnp.stack(mix_list) * factor[..., None], axis=0)
    mixed = (numerator / denominator[..., None]).reshape(TILE_DEV, inner_width)
    inner = layer_norm(mixed, inner_gain).astype(jnp.bfloat16)
    return jnp.dot(inner, output_weight, preferred_element_type=jnp.float32).astype(jnp.bfloat16)


MESH = pl.DeviceIdType.MESH
PIECE = 3 * HEAD_DIM
HALF = 1024
NT = (((1,), (1,)), ((), ()))
TN = (((0,), (0,)), ((), ()))
F32 = jnp.float32
BF16 = jnp.bfloat16
MIB = 2**20


ROUTE = (4, 3, 5, 2, 6, 1, 7)
HALVES = 2
PARTS = 2


def encode_kernel(
    heads_hbm,
    stream_hbm,
    scale_hbm,
    gain_hbm,
    bias_hbm,
    embed_bias_hbm,
    slide_gain_hbm,
    head_weight_hbm,
    embed_weight_hbm,
    triple_weight_hbm,
    recv_ref,
    heads,
    stream,
    scale_ref,
    gain_ref,
    bias_ref,
    embed_bias_ref,
    slide_gain_ref,
    head_weight,
    embed_weight,
    triple_weight,
    outbox,
    load_sem,
    vector_sem,
    own_sem,
    send_sem,
    pass_sem,
    recv_sem,
):
    group = lax.axis_index("groups")
    me = lax.axis_index("seq")
    chip, core = me // 2, lax.rem(me, 2)
    sibling = 2 * chip + 1 - core
    chips = HEADS
    depth = head_weight.shape[0]
    part = depth // 4
    rows = heads.shape[0] // HALVES

    barrier = pltpu.get_barrier_semaphore()
    for off in range(1, chips):
        peer = 2 * lax.rem(chip + off, chips) + core
        pl.semaphore_signal(barrier, inc=1, device_id=(group, peer), device_id_type=MESH)
    pl.semaphore_signal(barrier, inc=1, device_id=(group, sibling), device_id_type=MESH)

    def load(source, target, first, count, sem):
        copy = pltpu.make_async_copy(
            source.at[pl.ds(first, count)], target.at[pl.ds(first, count)], load_sem.at[sem]
        )
        copy.start()
        return copy

    head_loads = [load(heads_hbm, heads, 0, rows, 0)]
    weight_loads = [
        load(head_weight_hbm, head_weight, i * part, part, 1 + i) for i in range(4)
    ]
    stream_loads = []
    vector_loads = []
    for place, (source, target) in enumerate(
        (
            (scale_hbm, scale_ref),
            (gain_hbm, gain_ref),
            (bias_hbm, bias_ref),
            (embed_bias_hbm, embed_bias_ref),
            (slide_gain_hbm, slide_gain_ref),
        )
    ):
        copy = pltpu.make_async_copy(source, target, vector_sem.at[place])
        copy.start()
        vector_loads.append(copy)

    inner = HEADS * HEAD_DIM
    sends = []
    owns = []
    for half in range(HALVES):
        low = half * rows
        head_loads[half].wait()
        blended = None
        for i in range(4):
            if half == 0:
                weight_loads[i].wait()
                if i == 0:
                    stream_loads.append(load(stream_hbm, stream, 0, rows, 5))
                    embed_load = load(embed_weight_hbm, embed_weight, 0, embed_weight.shape[0], 6)
                if i == 2:
                    triple_load = load(
                        triple_weight_hbm, triple_weight, 0, triple_weight.shape[0], 7
                    )
            term = jnp.dot(
                heads[low : low + rows, i * part : (i + 1) * part],
                head_weight[i * part : (i + 1) * part, :],
                preferred_element_type=F32,
            )
            blended = term if blended is None else blended + term
        if half == 0:
            for copy in vector_loads:
                copy.wait()
            scale = scale_ref[...].reshape(1, -1)
            gain = gain_ref[...].reshape(1, -1)
            bias = bias_ref[...].reshape(1, -1)
            embed_bias = embed_bias_ref[...].reshape(1, -1)
            slide_gain = slide_gain_ref[...].reshape(1, -1)
        stream_loads[half].wait()
        summed = stream[low : low + rows, :].astype(F32) + scale * blended
        embedding = (layer_norm(summed, gain) + bias).astype(BF16)
        if half == 0:
            embed_load.wait()
        slide_rows = (
            jnp.dot(embedding, embed_weight[...], preferred_element_type=F32) + embed_bias
        ).astype(BF16)
        normed = layer_norm(slide_rows.astype(F32), slide_gain).astype(BF16)
        if half == 0:
            triple_load.wait()
            head_loads.append(load(heads_hbm, heads, rows, rows, 8))
            stream_loads.append(load(stream_hbm, stream, rows, rows, 9))
        triple = jnp.dot(normed, triple_weight[...], preferred_element_type=F32)
        turned = triple.T.astype(BF16)
        for h in range(HEADS):
            for kind in range(3):
                first = kind * inner + h * HEAD_DIM
                outbox[half, h, kind * HEAD_DIM : (kind + 1) * HEAD_DIM, :] = turned[
                    first : first + HEAD_DIM, :
                ]
        if half == 0:
            pl.semaphore_wait(barrier, chips)
        for off in ROUTE + (0,):
            to = lax.rem(chip + off, chips)
            copy = pltpu.make_async_remote_copy(
                src_ref=outbox.at[half, to],
                dst_ref=recv_ref.at[me, half],
                send_sem=send_sem.at[half, off],
                recv_sem=recv_sem.at[me, half],
                device_id=(group, 2 * to + core if off else sibling),
                device_id_type=MESH,
            )
            copy.start()
            sends.append(copy)
        own = pltpu.make_async_copy(
            outbox.at[half, chip], recv_ref.at[me, half], own_sem.at[half]
        )
        own.start()
        owns.append(own)

    def arrival(source, half, sem):
        return pltpu.make_async_remote_copy(
            src_ref=recv_ref.at[source, half],
            dst_ref=recv_ref.at[source, half],
            send_sem=sem,
            recv_sem=recv_sem.at[source, half],
            device_id=(group, sibling),
            device_id_type=MESH,
        )

    for half in range(HALVES):
        for off in ROUTE:
            source = 2 * lax.rem(chip + chips - off, chips) + core
            onward = arrival(source, half, pass_sem.at[half, off])
            onward.wait_recv()
            onward.start()
            sends.append(onward)
    for half in range(HALVES):
        for off in range(chips):
            source = 2 * lax.rem(chip + chips - off, chips) + 1 - core
            arrival(source, half, pass_sem.at[half, 0]).wait_recv()
    for copy in sends:
        copy.wait_send()
    for own in owns:
        own.wait()


def shared_depth(index, shift):
    residue = (index + 8 - shift) & 7
    depth = jnp.where(residue & 4 != 0, 3, 4)
    depth = jnp.where(residue & 2 != 0, 2, depth)
    return jnp.where(residue & 1 != 0, 1, depth)


def attend(keys, queries, multiplicity):
    scaling = math.log2(math.e) / math.sqrt(HEAD_DIM)
    scores = [
        lax.dot_general(block, queries, NT, preferred_element_type=F32) for block in keys
    ]
    highest = scores[0].max(axis=0, keepdims=True)
    for block in scores[1:]:
        highest = jnp.maximum(highest, block.max(axis=0, keepdims=True))
    total = blended = None
    for block, values, times in zip(scores, keys, multiplicity):
        weights = jnp.exp2((block - highest) * scaling)
        if times is not None:
            weights = weights * times
        part_total = weights.sum(axis=0, keepdims=True)
        part = lax.dot_general(values, weights.astype(BF16), TN, preferred_element_type=F32)
        total = part_total if total is None else total + part_total
        blended = part if blended is None else blended + part
    return blended[2 * HEAD_DIM : PIECE, :] / total


def compact_kernel(counts_ref, pieces, near_ref, off_ref, far_ref, left, right):
    me = lax.axis_index("seq")
    head, side = me // 2, lax.rem(me, 2)
    parity = lax.rem(head, 2)
    slots = pieces.shape[1] * pieces.shape[3]
    unit = (
        lax.broadcasted_iota(jnp.int32, (slots, slots), 0)
        == lax.broadcasted_iota(jnp.int32, (slots, slots), 1)
    ).astype(BF16)
    right[...] = jnp.zeros_like(right)
    start = 0
    for d in range(pieces.shape[0]):
        block = jnp.concatenate([pieces[d, half] for half in range(HALVES)], axis=1)
        rows = lax.dot_general(unit, block, NT, preferred_element_type=F32)
        left[pl.ds(start, slots), :] = rows[:, :128]
        right[pl.ds(start, slots), : PIECE - 128] = rows[:, 128:]
        start = start + counts_ref[d]

    def pick(target, first, which):
        place = pl.ds(first + which, HALF // 2, stride=2)
        target[:, :128] = left[place, :].astype(BF16)
        target[:, 128:] = right[place, :].astype(BF16)

    pick(near_ref, side * HALF, parity)
    pick(off_ref, side * HALF, 1 - parity)
    pick(far_ref, (1 - side) * HALF, parity)


def as_queries(rows):
    lane = lax.broadcasted_iota(jnp.int32, (HALF // 2, 128), 1)
    kept = jnp.where(lane < HEAD_DIM, rows[:, :128].astype(F32), 0.0)
    moved = pltpu.roll(kept, HEAD_DIM, 1).astype(BF16)
    return jnp.concatenate([moved, jnp.zeros_like(moved)], axis=1)


def attention_kernel(
    near_ref,
    off_ref,
    far_ref,
    gain_ref,
    weight_ref,
    out_ref,
    tiles_ref,
    inbox,
    own_sem,
    send_sem,
    recv_sem,
):
    group = lax.axis_index("groups")
    me = lax.axis_index("seq")
    head, side = me // 2, lax.rem(me, 2)
    parity, shift = lax.rem(head, 2), head // 2
    home_side = me // HEADS
    barrier = pltpu.get_barrier_semaphore()
    for h in range(HEADS):

        @pl.when(2 * h + home_side != me)
        def _():
            pl.semaphore_signal(
                barrier, inc=1, device_id=(group, 2 * h + home_side), device_id_type=MESH
            )

    def remote(t):
        return pltpu.make_async_remote_copy(
            src_ref=tiles_ref.at[t],
            dst_ref=inbox.at[head],
            send_sem=send_sem.at[t],
            recv_sem=recv_sem.at[head],
            device_id=(group, side * HEADS + t),
            device_id_type=MESH,
        )

    near, near_off, far = near_ref[...], off_ref[...], far_ref[...]
    count = HALF // 2
    key_depth = shared_depth(lax.broadcasted_iota(jnp.int32, (count, 1), 0), shift)
    query_depth = shared_depth(lax.broadcasted_iota(jnp.int32, (1, count), 1), shift)
    times = jnp.minimum(key_depth, query_depth).astype(F32)
    near_queries, off_queries = as_queries(near), as_queries(near_off)
    per = TILE_DEV // 2
    span = count // PARTS
    for part in range(PARTS):
        low = part * span
        part_times = times[:, low : low + span]
        same = attend(
            [near, near_off, far],
            near_queries[low : low + span, :],
            [part_times + 1.0, None, part_times],
        )
        off = attend([near, near_off], off_queries[low : low + span, :], [None, None])
        even = jnp.where(parity == 0, same, off).astype(BF16)
        odd = jnp.where(parity == 0, off, same).astype(BF16)
        if part == 0:
            pl.semaphore_wait(barrier, HEADS - jnp.where(side == home_side, 1, 0))
        for place in range(span // per):
            t = part * (span // per) + place
            tiles_ref[t] = jnp.concatenate(
                [
                    even[:, place * per : (place + 1) * per],
                    odd[:, place * per : (place + 1) * per],
                ],
                axis=1,
            )

            @pl.when(side * HEADS + t != me)
            def _():
                remote(t).start()

            @pl.when(side * HEADS + t == me)
            def _():
                own = pltpu.make_async_copy(tiles_ref.at[t], inbox.at[head], own_sem)
                own.start()
                own.wait()

    for h in range(HEADS):

        @pl.when(2 * h + home_side != me)
        def _():
            pltpu.make_async_remote_copy(
                src_ref=tiles_ref.at[0],
                dst_ref=inbox.at[h],
                send_sem=send_sem.at[0],
                recv_sem=recv_sem.at[h],
                device_id=(group, 2 * h + home_side),
                device_id_type=MESH,
            ).wait_recv()

    mixed = inbox[...].astype(F32).reshape(HEADS * HEAD_DIM, TILE_DEV)
    average = jnp.mean(mixed, axis=0, keepdims=True)
    centred = mixed - average
    spread = jnp.mean(centred * centred, axis=0, keepdims=True)
    inner = (centred * lax.rsqrt(spread + EPSILON) * gain_ref[...]).astype(BF16)
    row = lax.broadcasted_iota(jnp.int32, (TILE_DEV, TILE_DEV), 0)
    lane = lax.broadcasted_iota(jnp.int32, (TILE_DEV, TILE_DEV), 1)
    half = TILE_DEV // 2
    order = (row == 2 * lax.rem(lane, half) + lane // half).astype(BF16)
    rows = lax.dot_general(order, inner, NT, preferred_element_type=F32).astype(BF16)
    out_ref[...] = jnp.dot(rows, weight_ref[...], preferred_element_type=F32).astype(BF16)
    for t in range(HEADS):

        @pl.when(side * HEADS + t != me)
        def _():
            remote(t).wait_send()


def local(
    tile_heads,
    tile_stream,
    tissue_counts,
    head_weight,
    stream_scale,
    final_gain,
    final_bias,
    embed_weight,
    embed_bias,
    slide_gain,
    triple_weight,
    inner_gain,
    output_weight,
):
    devices = lax.axis_size("seq")
    if devices != 2 * HEADS:
        return local_general(
            tile_heads,
            tile_stream,
            tissue_counts,
            head_weight,
            stream_scale,
            final_gain,
            final_bias,
            embed_weight,
            embed_bias,
            slide_gain,
            triple_weight,
            inner_gain,
            output_weight,
        )
    slots = tile_heads.shape[0]
    vmem = pl.BlockSpec(memory_space=pltpu.VMEM)
    smem = pl.BlockSpec(memory_space=pltpu.SMEM)
    anywhere = pl.BlockSpec(memory_space=pl.ANY)
    dma = pltpu.SemaphoreType.DMA
    pieces = pl.pallas_call(
        encode_kernel,
        out_shape=jax.ShapeDtypeStruct((devices, HALVES, PIECE, slots // HALVES), BF16),
        in_specs=[anywhere] * 10,
        out_specs=anywhere,
        scratch_shapes=[
            pltpu.VMEM(tile_heads.shape, BF16),
            pltpu.VMEM(tile_stream.shape, BF16),
            pltpu.VMEM(stream_scale.shape, F32),
            pltpu.VMEM(final_gain.shape, F32),
            pltpu.VMEM(final_bias.shape, F32),
            pltpu.VMEM(embed_bias.shape, F32),
            pltpu.VMEM(slide_gain.shape, F32),
            pltpu.VMEM(head_weight.shape, BF16),
            pltpu.VMEM(embed_weight.shape, BF16),
            pltpu.VMEM(triple_weight.shape, BF16),
            pltpu.VMEM((HALVES, HEADS, PIECE, slots // HALVES), BF16),
            dma((10,)),
            dma((5,)),
            dma((HALVES,)),
            dma((HALVES, HEADS)),
            dma((HALVES, HEADS)),
            dma((devices, HALVES)),
        ],
        compiler_params=pltpu.CompilerParams(
            collective_id=0, has_side_effects=True, vmem_limit_bytes=56 * MIB
        ),
    )(
        tile_heads,
        tile_stream,
        stream_scale,
        final_gain,
        final_bias,
        embed_bias,
        slide_gain,
        head_weight,
        embed_weight,
        triple_weight,
    )
    listed = jax.ShapeDtypeStruct((HALF // 2, 256), BF16)
    near, off, far = pl.pallas_call(
        compact_kernel,
        out_shape=(listed, listed, listed),
        in_specs=[smem, vmem],
        out_specs=(vmem, vmem, vmem),
        scratch_shapes=[
            pltpu.VMEM((2 * HALF + slots, 128), F32),
            pltpu.VMEM((2 * HALF + slots, 128), F32),
        ],
        compiler_params=pltpu.CompilerParams(vmem_limit_bytes=24 * MIB),
    )(tissue_counts, pieces)
    return pl.pallas_call(
        attention_kernel,
        out_shape=jax.ShapeDtypeStruct((TILE_DEV, output_weight.shape[1]), BF16),
        in_specs=[vmem] * 5,
        out_specs=vmem,
        scratch_shapes=[
            pltpu.VMEM((HEADS, HEAD_DIM, TILE_DEV), BF16),
            pltpu.VMEM((HEADS, HEAD_DIM, TILE_DEV), BF16),
            dma,
            dma((HEADS,)),
            dma((HEADS,)),
        ],
        compiler_params=pltpu.CompilerParams(
            collective_id=1, has_side_effects=True, vmem_limit_bytes=32 * MIB
        ),
    )(near, off, far, inner_gain[:, None], output_weight)


def solution(mesh):
    placed = (
        P(("groups", "seq"), None),
        P(("groups", "seq"), None),
        P("groups"),
        P(),
        P(),
        P(),
        P(),
        P(),
        P(),
        P(),
        P(),
        P(),
        P(),
    )
    return jax.shard_map(
        local, mesh=mesh, in_specs=placed, out_specs=P(("groups", "seq"), None), check_vma=False
    )
```

```python
import math

import jax
import jax.numpy as jnp
import numpy as np
from jax import lax
from jax.experimental import pallas as pl
from jax.experimental.pallas import tpu as pltpu
from jax.sharding import PartitionSpec as P

HEAD_DIM = 48
HEADS = 8
BRANCHES = 5
SEG_BASE = 1024
TILE_DEV = 128


EPSILON = 1e-06
NEGATIVE = -1e30


def swapped(block, axis, stride):
    count = lax.axis_size(axis)
    route = []
    for low in range(count):
        high = low | 1 << stride
        if high != low and high < count:
            route += [(low, high), (high, low)]
    return lax.ppermute(block, axis, route)


def layer_norm(values, gain_vector):
    average = jnp.mean(values, axis=-1, keepdims=True)
    centred = values - average
    spread = jnp.mean(centred * centred, axis=-1, keepdims=True)
    return centred * lax.rsqrt(spread + EPSILON) * gain_vector


def encode(head_rows, stream_rows, head_weight, stream_scale, final_gain, final_bias):
    blended = jnp.dot(head_rows, head_weight, preferred_element_type=jnp.float32)
    summed = stream_rows.astype(jnp.float32) + stream_scale * blended
    return (layer_norm(summed, final_gain) + final_bias).astype(jnp.bfloat16)


def project(embedding, embed_weight, embed_bias):
    return (
        jnp.dot(embedding, embed_weight, preferred_element_type=jnp.float32) + embed_bias
    ).astype(jnp.bfloat16)


def member_table(stride):
    return np.arange(stride)[:, None] == (np.arange(HEADS) % stride)[None, :]


def select_heads(source, stride):
    shaped = source.reshape(source.shape[0] // stride, stride, HEADS, source.shape[-1])
    member = member_table(stride)[None, :, :, None]
    return jnp.sum(jnp.where(member, shaped, jnp.zeros((), shaped.dtype)), axis=1)


def spread_heads(values, stride, fill_value):
    member = member_table(stride)
    if values.ndim == 3:
        member = member[:, :, None]
    member = member[None]
    placed = jnp.where(member, values[:, None], jnp.asarray(fill_value, values.dtype))
    return placed.reshape((values.shape[0] * stride,) + values.shape[1:])


def local_general(
    tile_heads,
    tile_stream,
    tissue_counts,
    head_weight,
    stream_scale,
    final_gain,
    final_bias,
    embed_weight,
    embed_bias,
    slide_gain,
    triple_weight,
    inner_gain,
    output_weight,
):
    devices = lax.axis_size("seq")
    rank_here = lax.axis_index("seq")
    capacity = tile_heads.shape[0] // devices
    per_peer = TILE_DEV // devices
    starts = jnp.cumsum(tissue_counts) - tissue_counts
    own_start = starts[rank_here]

    def outbound(source):
        shaped = source.reshape(capacity, devices, source.shape[-1])
        return jnp.roll(shaped, own_start % devices, axis=1)

    column = jnp.remainder(rank_here - starts, devices)
    slot_ids = jnp.arange(capacity, dtype=jnp.int32)[:, None] * devices + column[None, :]
    filled = slot_ids < tissue_counts[None, :]
    home_slot = (starts[None, :] + slot_ids) // devices
    target = jnp.where(filled, home_slot, TILE_DEV).reshape(capacity * devices)

    def place_rows(arrived):
        flattened = arrived.reshape(capacity * devices, arrived.shape[-1])
        return (
            jnp.zeros((TILE_DEV, flattened.shape[-1]), flattened.dtype)
            .at[target]
            .set(flattened, mode="drop")
        )

    head_in, stream_in = (
        lax.all_to_all(outbound(tile_heads), "seq", split_axis=1, concat_axis=1, tiled=True),
        lax.all_to_all(outbound(tile_stream), "seq", split_axis=1, concat_axis=1, tiled=True),
    )
    embedding = encode(
        place_rows(head_in),
        place_rows(stream_in),
        head_weight,
        stream_scale,
        final_gain,
        final_bias,
    )
    back_home = lax.all_to_all(
        embedding.reshape(devices, per_peer, 1, embedding.shape[-1]),
        "seq",
        split_axis=0,
        concat_axis=2,
        tiled=True,
    )
    slide_rows = project(back_home.reshape(TILE_DEV, embedding.shape[-1]), embed_weight, embed_bias)
    normed = layer_norm(slide_rows.astype(jnp.float32), slide_gain).astype(jnp.bfloat16)
    triple = jnp.dot(normed, triple_weight, preferred_element_type=jnp.float32).astype(jnp.bfloat16)
    inner_width = HEADS * HEAD_DIM
    queries = triple[:, :inner_width].reshape(TILE_DEV, HEADS, HEAD_DIM)
    key_value = jnp.concatenate(
        [
            triple[:, inner_width : 2 * inner_width].reshape(TILE_DEV, HEADS, HEAD_DIM),
            triple[:, 2 * inner_width :].reshape(TILE_DEV, HEADS, HEAD_DIM),
        ],
        axis=2,
    )
    total_rows = TILE_DEV * devices
    strides = [2**branch for branch in range(BRANCHES)]
    depths = [
        (min(SEG_BASE * stride, total_rows) // TILE_DEV).bit_length() - 1 for stride in strides
    ]
    blocks = [
        select_heads(key_value, stride).reshape(TILE_DEV // stride, 2 * inner_width)
        for stride in strides
    ]
    gathered = []
    for branch in range(BRANCHES):
        current = blocks[branch]
        for bit_place in range(depths[branch]):
            partner = swapped(current, "seq", bit_place)
            current = jnp.concatenate([current, partner], axis=0)
        gathered.append(current)
    scaling = 1.0 / math.sqrt(HEAD_DIM)
    high_list, total_list, mix_list = ([], [], [])
    for branch in range(BRANCHES):
        stride = strides[branch]
        own_queries = select_heads(queries, stride)
        gathered_rows = gathered[branch].reshape(-1, HEADS, 2 * HEAD_DIM)
        scores = (
            jnp.einsum(
                "qhd,khd->hqk",
                own_queries,
                gathered_rows[:, :, :HEAD_DIM],
                preferred_element_type=jnp.float32,
            )
            * scaling
        )
        highest = jnp.max(scores, axis=2)
        weights = jnp.exp(scores - highest[:, :, None])
        summed = jnp.sum(weights, axis=2)
        blended = jnp.einsum(
            "hqk,khd->qhd",
            weights.astype(jnp.bfloat16),
            gathered_rows[:, :, HEAD_DIM:],
            preferred_element_type=jnp.float32,
        )
        high_list.append(spread_heads(highest.T, stride, NEGATIVE))
        total_list.append(spread_heads(summed.T, stride, 0.0))
        mix_list.append(spread_heads(blended, stride, 0.0))
    high_all = jnp.stack(high_list)
    summit = jnp.max(high_all, axis=0)
    factor = jnp.exp(high_all - summit)
    denominator = jnp.sum(jnp.stack(total_list) * factor, axis=0)
    numerator = jnp.sum(jnp.stack(mix_list) * factor[..., None], axis=0)
    mixed = (numerator / denominator[..., None]).reshape(TILE_DEV, inner_width)
    inner = layer_norm(mixed, inner_gain).astype(jnp.bfloat16)
    return jnp.dot(inner, output_weight, preferred_element_type=jnp.float32).astype(jnp.bfloat16)


MESH = pl.DeviceIdType.MESH
PIECE = 3 * HEAD_DIM
HALF = 1024
NT = (((1,), (1,)), ((), ()))
TN = (((0,), (0,)), ((), ()))
F32 = jnp.float32
BF16 = jnp.bfloat16
MIB = 2**20


ROUTE = (4, 3, 5, 2, 6, 1, 7)
HALVES = 2
PARTS = 2


def encode_kernel(
    heads_hbm,
    stream_hbm,
    scale_hbm,
    gain_hbm,
    bias_hbm,
    embed_bias_hbm,
    slide_gain_hbm,
    head_weight_hbm,
    embed_weight_hbm,
    triple_weight_hbm,
    recv_ref,
    heads,
    stream,
    scale_ref,
    gain_ref,
    bias_ref,
    embed_bias_ref,
    slide_gain_ref,
    head_weight,
    embed_weight,
    triple_weight,
    outbox,
    load_sem,
    vector_sem,
    own_sem,
    send_sem,
    pass_sem,
    recv_sem,
):
    group = lax.axis_index("groups")
    me = lax.axis_index("seq")
    chip, core = me // 2, lax.rem(me, 2)
    sibling = 2 * chip + 1 - core
    chips = HEADS
    depth = head_weight.shape[0]
    part = depth // 4
    rows = heads.shape[0] // HALVES

    barrier = pltpu.get_barrier_semaphore()
    for off in range(1, chips):
        peer = 2 * lax.rem(chip + off, chips) + core
        pl.semaphore_signal(barrier, inc=1, device_id=(group, peer), device_id_type=MESH)
    pl.semaphore_signal(barrier, inc=1, device_id=(group, sibling), device_id_type=MESH)

    def load(source, target, first, count, sem):
        copy = pltpu.make_async_copy(
            source.at[pl.ds(first, count)], target.at[pl.ds(first, count)], load_sem.at[sem]
        )
        copy.start()
        return copy

    head_loads = [load(heads_hbm, heads, 0, rows, 0)]
    weight_loads = [
        load(head_weight_hbm, head_weight, i * part, part, 1 + i) for i in range(4)
    ]
    stream_loads = []
    vector_loads = []
    for place, (source, target) in enumerate(
        (
            (scale_hbm, scale_ref),
            (gain_hbm, gain_ref),
            (bias_hbm, bias_ref),
            (embed_bias_hbm, embed_bias_ref),
            (slide_gain_hbm, slide_gain_ref),
        )
    ):
        copy = pltpu.make_async_copy(source, target, vector_sem.at[place])
        copy.start()
        vector_loads.append(copy)

    inner = HEADS * HEAD_DIM
    sends = []
    owns = []
    for half in range(HALVES):
        low = half * rows
        head_loads[half].wait()
        blended = None
        for i in range(4):
            if half == 0:
                weight_loads[i].wait()
                if i == 0:
                    stream_loads.append(load(stream_hbm, stream, 0, rows, 5))
                    embed_load = load(embed_weight_hbm, embed_weight, 0, embed_weight.shape[0], 6)
                if i == 2:
                    triple_load = load(
                        triple_weight_hbm, triple_weight, 0, triple_weight.shape[0], 7
                    )
            term = jnp.dot(
                heads[low : low + rows, i * part : (i + 1) * part],
                head_weight[i * part : (i + 1) * part, :],
                preferred_element_type=F32,
            )
            blended = term if blended is None else blended + term
        if half == 0:
            for copy in vector_loads:
                copy.wait()
            scale = scale_ref[...].reshape(1, -1)
            gain = gain_ref[...].reshape(1, -1)
            bias = bias_ref[...].reshape(1, -1)
            embed_bias = embed_bias_ref[...].reshape(1, -1)
            slide_gain = slide_gain_ref[...].reshape(1, -1)
        stream_loads[half].wait()
        summed = stream[low : low + rows, :].astype(F32) + scale * blended
        embedding = (layer_norm(summed, gain) + bias).astype(BF16)
        if half == 0:
            embed_load.wait()
        slide_rows = (
            jnp.dot(embedding, embed_weight[...], preferred_element_type=F32) + embed_bias
        ).astype(BF16)
        normed = layer_norm(slide_rows.astype(F32), slide_gain).astype(BF16)
        if half == 0:
            triple_load.wait()
            head_loads.append(load(heads_hbm, heads, rows, rows, 8))
            stream_loads.append(load(stream_hbm, stream, rows, rows, 9))
        triple = jnp.dot(normed, triple_weight[...], preferred_element_type=F32)
        turned = triple.T.astype(BF16)
        for h in range(HEADS):
            for kind in range(3):
                first = kind * inner + h * HEAD_DIM
                outbox[half, h, kind * HEAD_DIM : (kind + 1) * HEAD_DIM, :] = turned[
                    first : first + HEAD_DIM, :
                ]
        if half == 0:
            pl.semaphore_wait(barrier, chips)
        for off in ROUTE + (0,):
            to = lax.rem(chip + off, chips)
            copy = pltpu.make_async_remote_copy(
                src_ref=outbox.at[half, to],
                dst_ref=recv_ref.at[me, half],
                send_sem=send_sem.at[half, off],
                recv_sem=recv_sem.at[me, half],
                device_id=(group, 2 * to + core if off else sibling),
                device_id_type=MESH,
            )
            copy.start()
            sends.append(copy)
        own = pltpu.make_async_copy(
            outbox.at[half, chip], recv_ref.at[me, half], own_sem.at[half]
        )
        own.start()
        owns.append(own)

    def arrival(source, half, sem):
        return pltpu.make_async_remote_copy(
            src_ref=recv_ref.at[source, half],
            dst_ref=recv_ref.at[source, half],
            send_sem=sem,
            recv_sem=recv_sem.at[source, half],
            device_id=(group, sibling),
            device_id_type=MESH,
        )

    for half in range(HALVES):
        for off in ROUTE:
            source = 2 * lax.rem(chip + chips - off, chips) + core
            onward = arrival(source, half, pass_sem.at[half, off])
            onward.wait_recv()
            onward.start()
            sends.append(onward)
    for half in range(HALVES):
        for off in range(chips):
            source = 2 * lax.rem(chip + chips - off, chips) + 1 - core
            arrival(source, half, pass_sem.at[half, 0]).wait_recv()
    for copy in sends:
        copy.wait_send()
    for own in owns:
        own.wait()


def shared_depth(index, shift):
    residue = (index + 8 - shift) & 7
    depth = jnp.where(residue & 4 != 0, 3, 4)
    depth = jnp.where(residue & 2 != 0, 2, depth)
    return jnp.where(residue & 1 != 0, 1, depth)


def attend(keys, turned, queries, multiplicity):
    scaling = math.log2(math.e) / math.sqrt(HEAD_DIM)
    scores = [
        lax.dot_general(block, queries, NT, preferred_element_type=F32) for block in keys
    ]
    highest = scores[0].max(axis=0, keepdims=True)
    for block in scores[1:]:
        highest = jnp.maximum(highest, block.max(axis=0, keepdims=True))
    total = blended = None
    for block, values, times in zip(scores, turned, multiplicity):
        weights = jnp.exp2((block - highest) * scaling)
        if times is not None:
            weights = weights * times
        part_total = weights.sum(axis=0, keepdims=True)
        part = jnp.dot(values, weights.astype(BF16), preferred_element_type=F32)
        total = part_total if total is None else total + part_total
        blended = part if blended is None else blended + part
    return blended / total


def compact_kernel(counts_ref, pieces, near_ref, off_ref, far_ref, left, right):
    me = lax.axis_index("seq")
    head, side = me // 2, lax.rem(me, 2)
    parity = lax.rem(head, 2)
    slots = pieces.shape[1] * pieces.shape[3]
    unit = (
        lax.broadcasted_iota(jnp.int32, (slots, slots), 0)
        == lax.broadcasted_iota(jnp.int32, (slots, slots), 1)
    ).astype(BF16)
    right[...] = jnp.zeros_like(right)
    start = 0
    for d in range(pieces.shape[0]):
        block = jnp.concatenate([pieces[d, half] for half in range(HALVES)], axis=1)
        rows = lax.dot_general(unit, block, NT, preferred_element_type=F32)
        left[pl.ds(start, slots), :] = rows[:, :128]
        right[pl.ds(start, slots), : PIECE - 128] = rows[:, 128:]
        start = start + counts_ref[d]

    def pick(target, first, which):
        place = pl.ds(first + which, HALF // 2, stride=2)
        target[:, :128] = left[place, :].astype(BF16)
        target[:, 128:] = right[place, :].astype(BF16)

    pick(near_ref, side * HALF, parity)
    pick(off_ref, side * HALF, 1 - parity)
    pick(far_ref, (1 - side) * HALF, parity)


def as_queries(rows):
    lane = lax.broadcasted_iota(jnp.int32, (HALF // 2, 128), 1)
    kept = jnp.where(lane < HEAD_DIM, rows[:, :128].astype(F32), 0.0)
    moved = pltpu.roll(kept, HEAD_DIM, 1).astype(BF16)
    return jnp.concatenate([moved, jnp.zeros_like(moved)], axis=1)


def attention_kernel(
    near_ref,
    off_ref,
    far_ref,
    gain_ref,
    weight_ref,
    out_ref,
    tiles_ref,
    inbox,
    own_sem,
    send_sem,
    recv_sem,
):
    group = lax.axis_index("groups")
    me = lax.axis_index("seq")
    head, side = me // 2, lax.rem(me, 2)
    parity, shift = lax.rem(head, 2), head // 2
    home_side = me // HEADS
    barrier = pltpu.get_barrier_semaphore()
    for h in range(HEADS):

        @pl.when(2 * h + home_side != me)
        def _():
            pl.semaphore_signal(
                barrier, inc=1, device_id=(group, 2 * h + home_side), device_id_type=MESH
            )

    def remote(t):
        return pltpu.make_async_remote_copy(
            src_ref=tiles_ref.at[t],
            dst_ref=inbox.at[head],
            send_sem=send_sem.at[t],
            recv_sem=recv_sem.at[head],
            device_id=(group, side * HEADS + t),
            device_id_type=MESH,
        )

    near, near_off, far = near_ref[...], off_ref[...], far_ref[...]
    count = HALF // 2
    key_depth = shared_depth(lax.broadcasted_iota(jnp.int32, (count, 1), 0), shift)
    query_depth = shared_depth(lax.broadcasted_iota(jnp.int32, (1, count), 1), shift)
    times = jnp.minimum(key_depth, query_depth).astype(F32)
    near_queries, off_queries = as_queries(near), as_queries(near_off)
    near_t, off_t, far_t = [rows.T[2 * HEAD_DIM : PIECE, :] for rows in (near, near_off, far)]
    per = TILE_DEV // 2
    span = count // PARTS
    for part in range(PARTS):
        low = part * span
        part_times = times[:, low : low + span]
        same = attend(
            [near, near_off, far],
            [near_t, off_t, far_t],
            near_queries[low : low + span, :],
            [part_times + 1.0, None, part_times],
        )
        off = attend(
            [near, near_off], [near_t, off_t], off_queries[low : low + span, :], [None, None]
        )
        even = jnp.where(parity == 0, same, off).astype(BF16)
        odd = jnp.where(parity == 0, off, same).astype(BF16)
        if part == 0:
            pl.semaphore_wait(barrier, HEADS - jnp.where(side == home_side, 1, 0))
        for place in range(span // per):
            t = part * (span // per) + place
            tiles_ref[t] = jnp.concatenate(
                [
                    even[:, place * per : (place + 1) * per],
                    odd[:, place * per : (place + 1) * per],
                ],
                axis=1,
            )

            @pl.when(side * HEADS + t != me)
            def _():
                remote(t).start()

            @pl.when(side * HEADS + t == me)
            def _():
                own = pltpu.make_async_copy(tiles_ref.at[t], inbox.at[head], own_sem)
                own.start()
                own.wait()

    for h in range(HEADS):

        @pl.when(2 * h + home_side != me)
        def _():
            pltpu.make_async_remote_copy(
                src_ref=tiles_ref.at[0],
                dst_ref=inbox.at[h],
                send_sem=send_sem.at[0],
                recv_sem=recv_sem.at[h],
                device_id=(group, 2 * h + home_side),
                device_id_type=MESH,
            ).wait_recv()

    mixed = inbox[...].astype(F32).reshape(HEADS * HEAD_DIM, TILE_DEV)
    average = jnp.mean(mixed, axis=0, keepdims=True)
    centred = mixed - average
    spread = jnp.mean(centred * centred, axis=0, keepdims=True)
    inner = (centred * lax.rsqrt(spread + EPSILON) * gain_ref[...]).astype(BF16)
    row = lax.broadcasted_iota(jnp.int32, (TILE_DEV, TILE_DEV), 0)
    lane = lax.broadcasted_iota(jnp.int32, (TILE_DEV, TILE_DEV), 1)
    half = TILE_DEV // 2
    order = (row == 2 * lax.rem(lane, half) + lane // half).astype(BF16)
    rows = lax.dot_general(order, inner, NT, preferred_element_type=F32).astype(BF16)
    out_ref[...] = jnp.dot(rows, weight_ref[...], preferred_element_type=F32).astype(BF16)
    for t in range(HEADS):

        @pl.when(side * HEADS + t != me)
        def _():
            remote(t).wait_send()


def local(
    tile_heads,
    tile_stream,
    tissue_counts,
    head_weight,
    stream_scale,
    final_gain,
    final_bias,
    embed_weight,
    embed_bias,
    slide_gain,
    triple_weight,
    inner_gain,
    output_weight,
):
    devices = lax.axis_size("seq")
    if devices != 2 * HEADS:
        return local_general(
            tile_heads,
            tile_stream,
            tissue_counts,
            head_weight,
            stream_scale,
            final_gain,
            final_bias,
            embed_weight,
            embed_bias,
            slide_gain,
            triple_weight,
            inner_gain,
            output_weight,
        )
    slots = tile_heads.shape[0]
    vmem = pl.BlockSpec(memory_space=pltpu.VMEM)
    smem = pl.BlockSpec(memory_space=pltpu.SMEM)
    anywhere = pl.BlockSpec(memory_space=pl.ANY)
    dma = pltpu.SemaphoreType.DMA
    pieces = pl.pallas_call(
        encode_kernel,
        out_shape=jax.ShapeDtypeStruct((devices, HALVES, PIECE, slots // HALVES), BF16),
        in_specs=[anywhere] * 10,
        out_specs=anywhere,
        scratch_shapes=[
            pltpu.VMEM(tile_heads.shape, BF16),
            pltpu.VMEM(tile_stream.shape, BF16),
            pltpu.VMEM(stream_scale.shape, F32),
            pltpu.VMEM(final_gain.shape, F32),
            pltpu.VMEM(final_bias.shape, F32),
            pltpu.VMEM(embed_bias.shape, F32),
            pltpu.VMEM(slide_gain.shape, F32),
            pltpu.VMEM(head_weight.shape, BF16),
            pltpu.VMEM(embed_weight.shape, BF16),
            pltpu.VMEM(triple_weight.shape, BF16),
            pltpu.VMEM((HALVES, HEADS, PIECE, slots // HALVES), BF16),
            dma((10,)),
            dma((5,)),
            dma((HALVES,)),
            dma((HALVES, HEADS)),
            dma((HALVES, HEADS)),
            dma((devices, HALVES)),
        ],
        compiler_params=pltpu.CompilerParams(
            collective_id=0, has_side_effects=True, vmem_limit_bytes=56 * MIB
        ),
    )(
        tile_heads,
        tile_stream,
        stream_scale,
        final_gain,
        final_bias,
        embed_bias,
        slide_gain,
        head_weight,
        embed_weight,
        triple_weight,
    )
    listed = jax.ShapeDtypeStruct((HALF // 2, 256), BF16)
    near, off, far = pl.pallas_call(
        compact_kernel,
        out_shape=(listed, listed, listed),
        in_specs=[smem, vmem],
        out_specs=(vmem, vmem, vmem),
        scratch_shapes=[
            pltpu.VMEM((2 * HALF + slots, 128), F32),
            pltpu.VMEM((2 * HALF + slots, 128), F32),
        ],
        compiler_params=pltpu.CompilerParams(vmem_limit_bytes=24 * MIB),
    )(tissue_counts, pieces)
    return pl.pallas_call(
        attention_kernel,
        out_shape=jax.ShapeDtypeStruct((TILE_DEV, output_weight.shape[1]), BF16),
        in_specs=[vmem] * 5,
        out_specs=vmem,
        scratch_shapes=[
            pltpu.VMEM((HEADS, HEAD_DIM, TILE_DEV), BF16),
            pltpu.VMEM((HEADS, HEAD_DIM, TILE_DEV), BF16),
            dma,
            dma((HEADS,)),
            dma((HEADS,)),
        ],
        compiler_params=pltpu.CompilerParams(
            collective_id=1, has_side_effects=True, vmem_limit_bytes=32 * MIB
        ),
    )(near, off, far, inner_gain[:, None], output_weight)


def solution(mesh):
    placed = (
        P(("groups", "seq"), None),
        P(("groups", "seq"), None),
        P("groups"),
        P(),
        P(),
        P(),
        P(),
        P(),
        P(),
        P(),
        P(),
        P(),
        P(),
    )
    return jax.shard_map(
        local, mesh=mesh, in_specs=placed, out_specs=P(("groups", "seq"), None), check_vma=False
    )
```
